32 devices in a mesh: dp: 4 (over y, x), head: 4 (over z), seq: 2 (over core).
Axes of the slice: x: 2, y: 2, z: 4, core: 2. Of those that a mesh axis runs over, the one named last changes fastest.
Arguments:
- q_dense: bfloat16 [4096, 8, 128], P(('dp', 'seq'), 'head'), parts along dimension 0, may hold values from -108 to 108
- k_dense: bfloat16 [4096, 8, 128], P(('dp', 'seq'), 'head'), parts along dimension 0, may hold values from -4 to 4
- v_dense: bfloat16 [4096, 8, 128], P(('dp', 'seq'), 'head'), parts along dimension 0, may hold values from -4 to 4
- q_expert: bfloat16 [4096, 12, 128], P(('dp', 'seq'), 'head'), parts along dimension 0, may hold values from -108 to 108
- k_expert: bfloat16 [4096, 12, 128], P(('dp', 'seq'), 'head'), parts along dimension 0, may hold values from -4 to 4
- v_expert: bfloat16 [4096, 12, 128], P(('dp', 'seq'), 'head'), parts along dimension 0, may hold values from -4 to 4
- gate_logit: bfloat16 [12, 4096], P('head', ('dp', 'seq')), parts along dimension 1, may hold values from -8 to 8
- selection: int32 [12, 256], P('head', 'dp'), parts along dimension 1, may hold values from 0 to 1023, as said below
Outputs:
- dense_out: bfloat16 [4096, 8, 128], P(('dp', 'seq'), 'head'), parts along dimension 0
- expert_out: bfloat16 [4096, 12, 128], P(('dp', 'seq'), 'head'), parts along dimension 0
The draws below stay inside these ranges and needn't reach their ends.
There are 4 independent parts, one for each index of `dp`. The reference program is written for one: setup_inputs(seed, part) draws one part's arguments, and reference() takes and returns one part's arrays. A program takes and returns all parts, laid end to end along the dimension named above; each array names one. Nothing has to cross between parts.
Inputs may be any that keep to these rules, and one draw needn't show every extreme that they name: `selection`: each row lists 64 distinct token positions in increasing order; every row holds the first and the last token.
All inputs are finite; a program needn't handle non-finite values.
Results may differ from the reference program's by a relative error of at most 0.0055.
Values may be sent and summed in bfloat16 or wider, within the bound.
A program may use at most 64 MiB of HBM per device.

```python
import math
import jax
import jax.numpy as jnp
from jax import lax

HS = 128
TOK_DEV = 512
DH = 8
EH = 12
TOKENS = 1024
SEL = 64


def choose_tokens(key):
    noise = jax.random.randint(jax.random.fold_in(key, 101), (EH, TOKENS), 0, 1024)
    blocks = TOKENS // TOK_DEV
    raised = jax.random.randint(jax.random.fold_in(key, 102), (EH, blocks), 0, 4) * 512
    raised = jnp.repeat(raised, TOK_DEV, axis=1, total_repeat_length=TOKENS)
    places = jnp.arange(TOKENS, dtype=jnp.int32)
    boundary = jnp.where((places == 0) | (places == TOKENS - 1), 4096, 0)
    score = (noise + raised + boundary[None, :]) * TOKENS + places[None, :]
    leading = jax.lax.top_k(score, SEL)[0]
    return jnp.sort(leading % TOKENS, axis=1).astype(jnp.int32)


def dense_pair(key):
    shape = (TOKENS, DH, HS)
    keys = jnp.clip(jax.random.normal(jax.random.fold_in(key, 201), shape, jnp.float32), -4.0, 4.0)
    query = jnp.clip(jax.random.normal(jax.random.fold_in(key, 202), shape, jnp.float32), -4.0, 4.0)
    return (query, keys)


def expert_pair(key):
    shape = (TOKENS, EH, HS)
    keys = jnp.clip(jax.random.normal(jax.random.fold_in(key, 301), shape, jnp.float32), -4.0, 4.0)
    query = jnp.clip(jax.random.normal(jax.random.fold_in(key, 302), shape, jnp.float32), -4.0, 4.0)
    return (query, keys)


def draw_q_dense(key, part):
    return dense_pair(key)[0].astype(jnp.bfloat16)


def draw_k_dense(key, part):
    return dense_pair(key)[1].astype(jnp.bfloat16)


def draw_q_expert(key, part):
    return expert_pair(key)[0].astype(jnp.bfloat16)


def draw_k_expert(key, part):
    return expert_pair(key)[1].astype(jnp.bfloat16)


def draw_selection(key, part):
    return choose_tokens(key)


def shard_levels(own_key, extent, cuts, least, high):
    def one(position, shards_of):
        heights = jax.random.uniform(jax.random.fold_in(jax.random.fold_in(own_key, 6), position), (shards_of,), jnp.float32, least / len(cuts), high / len(cuts))
        return jnp.repeat(jnp.exp(heights), extent[position] // shards_of).reshape((-1,) + (1,) * (len(extent) - position - 1))

    level = one(*cuts[0])
    for cut in cuts[1:]:
        level = level * one(*cut)
    return level


def normal_values(own_key, extent, spread, limit, cuts=(), kind=jnp.bfloat16):
    array = spread * jax.random.normal(own_key, extent, jnp.float32)
    if cuts:
        array = array * shard_levels(own_key, extent, cuts, -0.22, 0.18)
    return jnp.clip(array, -limit, limit).astype(kind)


def setup_inputs(seed: int = 0, part: int = 0) -> dict:
    key_list = jax.random.split(jax.random.key(seed), 9)
    own_keys = jax.random.split(jax.random.fold_in(key_list[8], part), 9)
    return {
        "q_dense": draw_q_dense(jax.random.fold_in(jax.random.fold_in(key_list[8], part), 71), part),
        "k_dense": draw_k_dense(jax.random.fold_in(jax.random.fold_in(key_list[8], part), 71), part),
        "v_dense": normal_values(own_keys[2], (TOKENS, DH, HS), 1.0, 4.0, ((0, 2), (1, 4))),
        "q_expert": draw_q_expert(jax.random.fold_in(jax.random.fold_in(key_list[8], part), 71), part),
        "k_expert": draw_k_expert(jax.random.fold_in(jax.random.fold_in(key_list[8], part), 71), part),
        "v_expert": normal_values(own_keys[5], (TOKENS, EH, HS), 1.0, 4.0, ((0, 2), (1, 4))),
        "gate_logit": normal_values(own_keys[6], (EH, TOKENS), 2.0, 8.0, ((0, 4), (1, 2))),
        "selection": draw_selection(jax.random.fold_in(jax.random.fold_in(key_list[8], part), 71), part),
    }


NEGATIVE = -1e+30

def attend(queries, query_rank, keys, values, key_rank):
    scores = jnp.dot(queries, keys.T, preferred_element_type=jnp.float32) * (1.0 / math.sqrt(HS))
    visible = key_rank[None, :] <= query_rank[:, None]
    scores = jnp.where(visible, scores, NEGATIVE)
    leading = lax.optimization_barrier(jnp.max(scores, axis=1, keepdims=True))
    weights = jnp.where(visible, jnp.exp(scores - leading), 0.0)
    total = lax.optimization_barrier(jnp.sum(weights, axis=1, keepdims=True))
    mixed = jnp.dot(weights.astype(jnp.bfloat16), values, preferred_element_type=jnp.float32)
    return mixed / total

def dense_head(queries, keys, values):
    block = math.gcd(TOKENS, 512)
    ranks = jnp.arange(TOKENS, dtype=jnp.int32)

    def one_block(index):
        offset = index * block
        part_q = lax.dynamic_slice_in_dim(queries, offset, block, 0)
        part_rank = lax.dynamic_slice_in_dim(ranks, offset, block, 0)
        return attend(part_q, part_rank, keys, values, ranks).astype(jnp.bfloat16)
    blocks = lax.map(one_block, jnp.arange(TOKENS // block, dtype=jnp.int32))
    return blocks.reshape(TOKENS, HS)

def reference(q_dense, k_dense, v_dense, q_expert, k_expert, v_expert, gate_logit, selection):
    dense_out = jnp.stack([dense_head(q_dense[:, head], k_dense[:, head], v_dense[:, head]) for head in range(DH)], axis=1)
    expert_out = jnp.zeros((TOKENS, EH, HS), jnp.bfloat16)
    ranks = jnp.arange(SEL, dtype=jnp.int32)
    for head in range(EH):
        chosen = selection[head]
        mixed = attend(q_expert[chosen, head], ranks, k_expert[chosen, head], v_expert[chosen, head], ranks)
        gate = jax.nn.sigmoid(gate_logit[head, chosen].astype(jnp.float32))
        expert_out = expert_out.at[chosen, head].set((mixed * gate[:, None]).astype(jnp.bfloat16))
    return (dense_out, expert_out)
```

```python
import math

import jax
import jax.numpy as jnp
from jax import lax
from jax.experimental import pallas as pl
from jax.experimental.pallas import tpu as pltpu
from jax.sharding import PartitionSpec as P

NEGATIVE = -1e30


def plain_rows(rows, tok_rows, count):
    return rows


def online_update(state, queries, query_pos, keys, values, key_pos, scale):
    leading, total, summed = state
    scores = jnp.einsum("qhd,khd->qhk", queries, keys, preferred_element_type=jnp.float32) * scale
    visible = key_pos[None, None, :] <= query_pos[:, None, None]
    scores = jnp.where(visible, scores, NEGATIVE)
    new_leading = jnp.maximum(leading, jnp.max(scores, axis=2))
    shrink = jnp.exp(leading - new_leading)
    weights = jnp.where(visible, jnp.exp(scores - new_leading[:, :, None]), 0.0)
    total = total * shrink + jnp.sum(weights, axis=2)
    moved = jnp.einsum(
        "qhk,khd->qhd", weights.astype(jnp.bfloat16), values, preferred_element_type=jnp.float32
    )
    return (new_leading, total, summed * shrink[:, :, None] + moved)


def dense_heads(queries, keys, values, position_map):
    tok_rows, heads, width = queries.shape
    count = lax.axis_size("seq")
    half_rows = tok_rows // 2
    own_rows = lax.axis_index("seq") * tok_rows + jnp.arange(tok_rows, dtype=jnp.int32)
    query_pos = position_map(own_rows, tok_rows, count).reshape(2, half_rows)
    groups = queries.reshape(2, half_rows, heads, width)
    scale = 1.0 / math.sqrt(width)
    blank = (
        jnp.full((half_rows, heads), NEGATIVE, jnp.float32),
        jnp.zeros((half_rows, heads), jnp.float32),
        jnp.zeros((half_rows, heads, width), jnp.float32),
    )
    key_rows = lax.all_gather(keys, "seq", axis=0, tiled=True)
    value_rows = lax.all_gather(values, "seq", axis=0, tiled=True)
    length = key_rows.shape[0]
    block = math.gcd(length, 512)
    count_blocks = length // block
    key_pos = position_map(jnp.arange(length, dtype=jnp.int32), tok_rows, count).reshape(
        count_blocks, block
    )
    key_blocks = key_rows.reshape(count_blocks, block, heads, width)
    value_blocks = value_rows.reshape(count_blocks, block, heads, width)

    def advance(state, item):
        key_block, value_block, block_pos = item
        result = []
        for group in range(2):
            seen = jnp.min(block_pos) <= jnp.max(query_pos[group])
            result.append(
                lax.cond(
                    seen,
                    lambda inner, member=group: online_update(
                        inner,
                        groups[member],
                        query_pos[member],
                        key_block,
                        value_block,
                        block_pos,
                        scale,
                    ),
                    lambda inner: inner,
                    state[group],
                )
            )
        return (tuple(result), None)

    final_state, unused = lax.scan(advance, (blank, blank), (key_blocks, value_blocks, key_pos))
    outputs = [
        (summed / total[:, :, None]).astype(jnp.bfloat16) for leading, total, summed in final_state
    ]
    return jnp.concatenate(outputs, axis=0)


def attend_ranked(query_rows, query_ranks, keys, values, gate_rows):
    heads, rows, width = query_rows.shape
    block = math.gcd(rows, 512)
    scale = 1.0 / math.sqrt(width)
    key_ranks = jnp.arange(keys.shape[1], dtype=jnp.int32)

    def one_block(index):
        scores = (
            jnp.einsum("erd,ekd->erk", query_rows, keys, preferred_element_type=jnp.float32) * scale
        )
        visible = key_ranks[None, None, :] <= query_ranks[:, :, None]
        scores = jnp.where(visible, scores, NEGATIVE)
        leading = jnp.max(scores, axis=2, keepdims=True)
        weights = jnp.where(visible, jnp.exp(scores - leading), 0.0)
        total = jnp.sum(weights, axis=2, keepdims=True)
        mixed = (
            jnp.einsum(
                "erk,ekd->erd",
                weights.astype(jnp.bfloat16),
                values,
                preferred_element_type=jnp.float32,
            )
            / total
        )
        return (mixed * jax.nn.sigmoid(gate_rows.astype(jnp.float32))[:, :, None]).astype(
            jnp.bfloat16
        )

    blocks = lax.map(one_block, jnp.arange(rows // block, dtype=jnp.int32))
    return jnp.moveaxis(blocks, 0, 1).reshape(heads, rows, width)


def sparse_heads(queries, keys, values, gate_logit, selection):
    tok_rows, heads, width = queries.shape
    chosen = selection.shape[1]
    start = lax.axis_index("seq") * tok_rows
    positions = start + jnp.arange(tok_rows, dtype=jnp.int32)
    matches = selection[:, :, None] == positions[None, None, :]
    one_hot = matches.astype(jnp.bfloat16)

    def pick(source):
        return jnp.einsum(
            "ent,ted->end", one_hot, source, preferred_element_type=jnp.float32
        ).astype(jnp.bfloat16)

    gate_rows = jnp.einsum("ent,et->en", one_hot, gate_logit, preferred_element_type=jnp.float32)
    gathered = (
        lax.psum(pick(queries), "seq").astype(jnp.float32),
        lax.psum(pick(keys), "seq").astype(jnp.float32),
        lax.psum(pick(values), "seq").astype(jnp.float32),
        lax.psum(gate_rows.astype(jnp.bfloat16), "seq").astype(jnp.float32),
    )
    picked_q, picked_k, picked_v, picked_gate = [member.astype(jnp.bfloat16) for member in gathered]
    all_ranks = jnp.broadcast_to(jnp.arange(chosen, dtype=jnp.int32)[None, :], (heads, chosen))
    results = attend_ranked(picked_q, all_ranks, picked_k, picked_v, picked_gate)
    return jnp.einsum("ent,end->ted", one_hot, results, preferred_element_type=jnp.float32).astype(
        jnp.bfloat16
    )


def local(q_dense, k_dense, v_dense, q_expert, k_expert, v_expert, gate_logit, selection):
    dense_out = dense_heads(q_dense, k_dense, v_dense, plain_rows)
    expert_out = sparse_heads(q_expert, k_expert, v_expert, gate_logit, selection)
    return (dense_out, expert_out)

def nearest_pair(tok_rows, heads, width, experts, chosen):
    scale = math.log2(math.e) / math.sqrt(width)
    block = tok_rows // 2
    contract_last = (((1,), (1,)), ((), ()))
    f32, bf16 = jnp.float32, jnp.bfloat16

    def kernel(
        q_ref, k_ref, v_ref, qe_ref, ke_ref, ve_ref, gate_ref, sel_ref,
        dense_ref, expert_ref,
        q_in, k_in, v_in, k_far, v_far, qe_in, ke_in, ve_in,
        wide, q_all, k_all, v_all, kf_all, vf_all, state, leading,
        picked, picked_far, in_sem, send_sem, recv_sem,
    ):
        me = lax.axis_index("seq")
        first = me == 0
        barrier = pltpu.get_barrier_semaphore()
        partner = {"seq": 1 - me}

        def far_copy(number, source, target):
            return pltpu.make_async_remote_copy(
                src_ref=source,
                dst_ref=target,
                send_sem=send_sem.at[number],
                recv_sem=recv_sem.at[number],
                device_id=partner,
                device_id_type=pl.DeviceIdType.MESH,
            )

        sent_k = far_copy(0, k_ref, k_far)
        sent_v = far_copy(1, v_ref, v_far)
        sent_picked = far_copy(2, picked, picked_far)

        @pl.when(me == 1)
        def _():
            pl.semaphore_signal(
                barrier, inc=1, device_id=partner, device_id_type=pl.DeviceIdType.MESH
            )

        loads = [
            pltpu.make_async_copy(source, target, in_sem.at[number])
            for number, (source, target) in enumerate(
                (
                    (ke_ref, ke_in),
                    (ve_ref, ve_in),
                    (k_ref, k_in),
                    (q_ref, q_in),
                    (v_ref, v_in),
                    (qe_ref, qe_in),
                )
            )
        ]
        for load in loads:
            load.start()

        @pl.when(first)
        def _():
            pl.semaphore_wait(barrier, 1)
            sent_k.start()
            sent_v.start()

        chosen_rows = sel_ref[...].astype(f32)
        start = (me * tok_rows).astype(f32)
        places = start + lax.broadcasted_iota(jnp.int32, (chosen, tok_rows), 1).astype(f32)
        one_hot = []
        for head in range(experts):
            square = jnp.broadcast_to(chosen_rows[head : head + 1, :], (chosen, chosen)).T
            one_hot.append(
                jnp.where(square[:, 0:1] == places, 1.0, 0.0).astype(bf16)
            )

        def pick(head, source):
            return jnp.dot(one_hot[head], source[head], preferred_element_type=f32).astype(bf16)

        loads[0].wait()
        for head in range(experts):
            picked[0, head] = pick(head, ke_in)
        loads[1].wait()
        for head in range(experts):
            picked[1, head] = pick(head, ve_in)

        @pl.when(first)
        def _():
            sent_picked.start()

        def split(source, number, target):
            wide[number] = source[...].astype(f32)
            for head in range(heads):
                target[head, :, 0:width] = wide[
                    number, pl.ds(head, tok_rows, stride=heads), :
                ].astype(bf16)

        ones = jnp.ones((tok_rows, width), bf16)
        for head in range(heads):
            v_all[head, :, width:] = ones
            vf_all[head, :, width:] = ones
        loads[2].wait()
        split(k_in, 0, k_all)
        loads[3].wait()
        split(q_in, 1, q_all)
        loads[4].wait()
        split(v_in, 2, v_all)

        for head in range(heads):
            for part in range(2):
                rows = slice(part * block, (part + 1) * block)
                seen = (part + 1) * block
                scores = lax.dot_general(
                    q_all[head, rows, :],
                    k_all[head, 0:seen, :],
                    contract_last,
                    preferred_element_type=f32,
                )
                row_pos = part * block + lax.broadcasted_iota(jnp.int32, (block, seen), 0)
                col_pos = lax.broadcasted_iota(jnp.int32, (block, seen), 1)
                scores = jnp.where(col_pos <= row_pos, scores, NEGATIVE)
                top = jnp.max(scores, axis=1, keepdims=True)
                weights = jnp.exp2((scores - top) * scale).astype(bf16)
                state[head, rows, :] = jnp.dot(
                    weights, v_all[head, 0:seen, :], preferred_element_type=f32
                )
                leading[head, rows, :] = jnp.broadcast_to(top, (block, width))

        @pl.when(me == 1)
        def _():
            sent_k.wait_recv()
            split(k_far, 0, kf_all)
            sent_v.wait_recv()
            split(v_far, 2, vf_all)
            for head in range(heads):
                for part in range(2):
                    rows = slice(part * block, (part + 1) * block)
                    scores = lax.dot_general(
                        q_all[head, rows, :],
                        kf_all[head],
                        contract_last,
                        preferred_element_type=f32,
                    )
                    old = leading[head, rows, 0:1]
                    top = jnp.maximum(old, jnp.max(scores, axis=1, keepdims=True))
                    weights = jnp.exp2((scores - top) * scale).astype(bf16)
                    state[head, rows, :] = state[head, rows, :] * jnp.exp2(
                        (old - top) * scale
                    ) + jnp.dot(weights, vf_all[head], preferred_element_type=f32)
            sent_picked.wait_recv()
            picked[...] = picked[...] + picked_far[...]

        for head in range(heads):
            wide[1, pl.ds(head, tok_rows, stride=heads), :] = (
                state[head, :, 0:width] / state[head, :, width:]
            )
        dense_ref[...] = wide[1].astype(bf16)

        loads[5].wait()
        token = start + lax.broadcasted_iota(jnp.int32, (tok_rows, chosen), 0).astype(f32)
        visible = lax.broadcasted_iota(jnp.int32, (chosen, chosen), 1) <= (
            lax.broadcasted_iota(jnp.int32, (chosen, chosen), 0)
        )
        for head in range(experts):
            query = pick(head, qe_in)
            logit = jnp.sum(
                one_hot[head].astype(f32) * gate_ref[head : head + 1, :].astype(f32),
                axis=1,
                keepdims=True,
            )
            scores = lax.dot_general(
                query, picked[0, head], contract_last, preferred_element_type=f32
            )
            scores = jnp.where(visible, scores, NEGATIVE)
            top = jnp.max(scores, axis=1, keepdims=True)
            weights = jnp.where(visible, jnp.exp2((scores - top) * scale), 0.0)
            total = jnp.sum(weights, axis=1, keepdims=True)
            mixed = (
                jnp.dot(weights.astype(bf16), picked[1, head], preferred_element_type=f32) / total
            )
            result = (mixed / (1.0 + jnp.exp(-logit))).astype(bf16)
            spread = jnp.where(chosen_rows[head : head + 1, :] == token, 1.0, 0.0).astype(bf16)
            expert_ref[head] = jnp.dot(spread, result, preferred_element_type=f32).astype(bf16)

        @pl.when(first)
        def _():
            sent_k.wait_send()
            sent_v.wait_send()
            sent_picked.wait_send()

    in_hbm = pl.BlockSpec(memory_space=pltpu.HBM)
    in_vmem = pl.BlockSpec(memory_space=pltpu.VMEM)
    flat = (tok_rows * heads, width)
    return pl.pallas_call(
        kernel,
        out_shape=(
            jax.ShapeDtypeStruct(flat, bf16),
            jax.ShapeDtypeStruct((experts, tok_rows, width), bf16),
        ),
        in_specs=[in_hbm] * 6 + [in_vmem] * 2,
        out_specs=(in_vmem, in_vmem),
        scratch_shapes=[pltpu.VMEM(flat, bf16)] * 5
        + [pltpu.VMEM((experts, tok_rows, width), bf16)] * 3
        + [
            pltpu.VMEM((3,) + flat, f32),
            pltpu.VMEM((heads, tok_rows, width), bf16),
            pltpu.VMEM((heads, tok_rows, width), bf16),
            pltpu.VMEM((heads, tok_rows, 2 * width), bf16),
            pltpu.VMEM((heads, tok_rows, width), bf16),
            pltpu.VMEM((heads, tok_rows, 2 * width), bf16),
            pltpu.VMEM((heads, tok_rows, 2 * width), f32),
            pltpu.VMEM((heads, tok_rows, width), f32),
            pltpu.VMEM((2, experts, chosen, width), bf16),
            pltpu.VMEM((2, experts, chosen, width), bf16),
            pltpu.SemaphoreType.DMA((6,)),
            pltpu.SemaphoreType.DMA((3,)),
            pltpu.SemaphoreType.DMA((3,)),
        ],
        compiler_params=pltpu.CompilerParams(
            collective_id=0, has_side_effects=True, vmem_limit_bytes=32 * 1024 * 1024
        ),
    )


def local_pair(q_dense, k_dense, v_dense, q_expert, k_expert, v_expert, gate_logit, selection):
    tok_rows, heads, width = q_dense.shape
    experts, chosen = selection.shape
    call = nearest_pair(tok_rows, heads, width, experts, chosen)
    dense_out, expert_out = call(
        *(member.reshape(tok_rows * heads, width) for member in (q_dense, k_dense, v_dense)),
        *(jnp.transpose(member, (1, 0, 2)) for member in (q_expert, k_expert, v_expert)),
        gate_logit,
        selection,
    )
    return (dense_out.reshape(tok_rows, heads, width), jnp.transpose(expert_out, (1, 0, 2)))


def solution(mesh):
    placed = (
        P(("dp", "seq"), "head", None),
        P(("dp", "seq"), "head", None),
        P(("dp", "seq"), "head", None),
        P(("dp", "seq"), "head", None),
        P(("dp", "seq"), "head", None),
        P(("dp", "seq"), "head", None),
        P("head", ("dp", "seq")),
        P("head", "dp"),
    )
    return jax.shard_map(
        local_pair if mesh.shape["seq"] == 2 else local,
        mesh=mesh,
        in_specs=placed,
        out_specs=(P(("dp", "seq"), "head", None), P(("dp", "seq"), "head", None)),
        check_vma=False,
    )
```

```python
import math

import jax
import jax.numpy as jnp
from jax import lax
from jax.experimental import pallas as pl
from jax.experimental.pallas import tpu as pltpu
from jax.sharding import PartitionSpec as P

NEGATIVE = -1e30


def plain_rows(rows, tok_rows, count):
    return rows


def online_update(state, queries, query_pos, keys, values, key_pos, scale):
    leading, total, summed = state
    scores = jnp.einsum("qhd,khd->qhk", queries, keys, preferred_element_type=jnp.float32) * scale
    visible = key_pos[None, None, :] <= query_pos[:, None, None]
    scores = jnp.where(visible, scores, NEGATIVE)
    new_leading = jnp.maximum(leading, jnp.max(scores, axis=2))
    shrink = jnp.exp(leading - new_leading)
    weights = jnp.where(visible, jnp.exp(scores - new_leading[:, :, None]), 0.0)
    total = total * shrink + jnp.sum(weights, axis=2)
    moved = jnp.einsum(
        "qhk,khd->qhd", weights.astype(jnp.bfloat16), values, preferred_element_type=jnp.float32
    )
    return (new_leading, total, summed * shrink[:, :, None] + moved)


def dense_heads(queries, keys, values, position_map):
    tok_rows, heads, width = queries.shape
    count = lax.axis_size("seq")
    half_rows = tok_rows // 2
    own_rows = lax.axis_index("seq") * tok_rows + jnp.arange(tok_rows, dtype=jnp.int32)
    query_pos = position_map(own_rows, tok_rows, count).reshape(2, half_rows)
    groups = queries.reshape(2, half_rows, heads, width)
    scale = 1.0 / math.sqrt(width)
    blank = (
        jnp.full((half_rows, heads), NEGATIVE, jnp.float32),
        jnp.zeros((half_rows, heads), jnp.float32),
        jnp.zeros((half_rows, heads, width), jnp.float32),
    )
    key_rows = lax.all_gather(keys, "seq", axis=0, tiled=True)
    value_rows = lax.all_gather(values, "seq", axis=0, tiled=True)
    length = key_rows.shape[0]
    block = math.gcd(length, 512)
    count_blocks = length // block
    key_pos = position_map(jnp.arange(length, dtype=jnp.int32), tok_rows, count).reshape(
        count_blocks, block
    )
    key_blocks = key_rows.reshape(count_blocks, block, heads, width)
    value_blocks = value_rows.reshape(count_blocks, block, heads, width)

    def advance(state, item):
        key_block, value_block, block_pos = item
        result = []
        for group in range(2):
            seen = jnp.min(block_pos) <= jnp.max(query_pos[group])
            result.append(
                lax.cond(
                    seen,
                    lambda inner, member=group: online_update(
                        inner,
                        groups[member],
                        query_pos[member],
                        key_block,
                        value_block,
                        block_pos,
                        scale,
                    ),
                    lambda inner: inner,
                    state[group],
                )
            )
        return (tuple(result), None)

    final_state, unused = lax.scan(advance, (blank, blank), (key_blocks, value_blocks, key_pos))
    outputs = [
        (summed / total[:, :, None]).astype(jnp.bfloat16) for leading, total, summed in final_state
    ]
    return jnp.concatenate(outputs, axis=0)


def attend_ranked(query_rows, query_ranks, keys, values, gate_rows):
    heads, rows, width = query_rows.shape
    block = math.gcd(rows, 512)
    scale = 1.0 / math.sqrt(width)
    key_ranks = jnp.arange(keys.shape[1], dtype=jnp.int32)

    def one_block(index):
        scores = (
            jnp.einsum("erd,ekd->erk", query_rows, keys, preferred_element_type=jnp.float32) * scale
        )
        visible = key_ranks[None, None, :] <= query_ranks[:, :, None]
        scores = jnp.where(visible, scores, NEGATIVE)
        leading = jnp.max(scores, axis=2, keepdims=True)
        weights = jnp.where(visible, jnp.exp(scores - leading), 0.0)
        total = jnp.sum(weights, axis=2, keepdims=True)
        mixed = (
            jnp.einsum(
                "erk,ekd->erd",
                weights.astype(jnp.bfloat16),
                values,
                preferred_element_type=jnp.float32,
            )
            / total
        )
        return (mixed * jax.nn.sigmoid(gate_rows.astype(jnp.float32))[:, :, None]).astype(
            jnp.bfloat16
        )

    blocks = lax.map(one_block, jnp.arange(rows // block, dtype=jnp.int32))
    return jnp.moveaxis(blocks, 0, 1).reshape(heads, rows, width)


def sparse_heads(queries, keys, values, gate_logit, selection):
    tok_rows, heads, width = queries.shape
    chosen = selection.shape[1]
    start = lax.axis_index("seq") * tok_rows
    positions = start + jnp.arange(tok_rows, dtype=jnp.int32)
    matches = selection[:, :, None] == positions[None, None, :]
    one_hot = matches.astype(jnp.bfloat16)

    def pick(source):
        return jnp.einsum(
            "ent,ted->end", one_hot, source, preferred_element_type=jnp.float32
        ).astype(jnp.bfloat16)

    gate_rows = jnp.einsum("ent,et->en", one_hot, gate_logit, preferred_element_type=jnp.float32)
    gathered = (
        lax.psum(pick(queries), "seq").astype(jnp.float32),
        lax.psum(pick(keys), "seq").astype(jnp.float32),
        lax.psum(pick(values), "seq").astype(jnp.float32),
        lax.psum(gate_rows.astype(jnp.bfloat16), "seq").astype(jnp.float32),
    )
    picked_q, picked_k, picked_v, picked_gate = [member.astype(jnp.bfloat16) for member in gathered]
    all_ranks = jnp.broadcast_to(jnp.arange(chosen, dtype=jnp.int32)[None, :], (heads, chosen))
    results = attend_ranked(picked_q, all_ranks, picked_k, picked_v, picked_gate)
    return jnp.einsum("ent,end->ted", one_hot, results, preferred_element_type=jnp.float32).astype(
        jnp.bfloat16
    )


def local(q_dense, k_dense, v_dense, q_expert, k_expert, v_expert, gate_logit, selection):
    dense_out = dense_heads(q_dense, k_dense, v_dense, plain_rows)
    expert_out = sparse_heads(q_expert, k_expert, v_expert, gate_logit, selection)
    return (dense_out, expert_out)

def nearest_pair(tok_rows, heads, width, experts, chosen):
    scale = math.log2(math.e) / math.sqrt(width)
    block = tok_rows // 2
    contract_last = (((1,), (1,)), ((), ()))
    f32, bf16 = jnp.float32, jnp.bfloat16

    def kernel(
        q_ref, k_ref, v_ref, qe_ref, ke_ref, ve_ref, gate_hbm, sel_hbm,
        dense_ref, expert_ref,
        q_in, k_in, v_in, k_far, v_far, qe_in, ke_in, ve_in,
        wide, q_all, k_all, v_all, kf_all, vf_all, state, leading,
        picked, picked_far, gate_ref, sel_ref, in_sem, send_sem, recv_sem,
    ):
        me = lax.axis_index("seq")
        first = me == 0
        barrier = pltpu.get_barrier_semaphore()
        partner = {"seq": 1 - me}

        def far_copy(number, source, target):
            return pltpu.make_async_remote_copy(
                src_ref=source,
                dst_ref=target,
                send_sem=send_sem.at[number],
                recv_sem=recv_sem.at[number],
                device_id=partner,
                device_id_type=pl.DeviceIdType.MESH,
            )

        sent_k = far_copy(0, k_ref, k_far)
        sent_v = far_copy(1, v_ref, v_far)
        sent_picked = far_copy(2, picked, picked_far)

        @pl.when(me == 1)
        def _():
            pl.semaphore_signal(
                barrier, inc=1, device_id=partner, device_id_type=pl.DeviceIdType.MESH
            )

        loads = [
            pltpu.make_async_copy(source, target, in_sem.at[number])
            for number, (source, target) in enumerate(
                (
                    (sel_hbm, sel_ref),
                    (ke_ref, ke_in),
                    (ve_ref, ve_in),
                    (k_ref, k_in),
                    (q_ref, q_in),
                    (v_ref, v_in),
                    (qe_ref, qe_in),
                    (gate_hbm, gate_ref),
                )
            )
        ]
        for load in loads:
            load.start()

        @pl.when(first)
        def _():
            pl.semaphore_wait(barrier, 1)
            sent_k.start()
            sent_v.start()

        loads[0].wait()
        chosen_rows = sel_ref[...].astype(f32)
        start = (me * tok_rows).astype(f32)
        places = start + lax.broadcasted_iota(jnp.int32, (chosen, tok_rows), 1).astype(f32)
        one_hot = []
        for head in range(experts):
            square = jnp.broadcast_to(chosen_rows[head : head + 1, :], (chosen, chosen)).T
            one_hot.append(
                jnp.where(square[:, 0:1] == places, 1.0, 0.0).astype(bf16)
            )

        def pick(head, source):
            return jnp.dot(one_hot[head], source[head], preferred_element_type=f32).astype(bf16)

        loads[1].wait()
        for head in range(experts):
            picked[0, head] = pick(head, ke_in)
        loads[2].wait()
        for head in range(experts):
            picked[1, head] = pick(head, ve_in)

        @pl.when(first)
        def _():
            sent_picked.start()

        def split(source, number, target):
            wide[number] = source[...].astype(f32)
            for head in range(heads):
                target[head, :, 0:width] = wide[
                    number, pl.ds(head, tok_rows, stride=heads), :
                ].astype(bf16)

        ones = jnp.ones((tok_rows, width), bf16)
        for head in range(heads):
            v_all[head, :, width:] = ones
            vf_all[head, :, width:] = ones
        loads[3].wait()
        split(k_in, 0, k_all)
        loads[4].wait()
        split(q_in, 1, q_all)
        loads[5].wait()
        split(v_in, 2, v_all)

        for head in range(heads):
            for part in range(2):
                rows = slice(part * block, (part + 1) * block)
                seen = (part + 1) * block
                scores = lax.dot_general(
                    q_all[head, rows, :],
                    k_all[head, 0:seen, :],
                    contract_last,
                    preferred_element_type=f32,
                )
                row_pos = part * block + lax.broadcasted_iota(jnp.int32, (block, seen), 0)
                col_pos = lax.broadcasted_iota(jnp.int32, (block, seen), 1)
                scores = jnp.where(col_pos <= row_pos, scores, NEGATIVE)
                top = jnp.max(scores, axis=1, keepdims=True)
                weights = jnp.exp2((scores - top) * scale).astype(bf16)
                state[head, rows, :] = jnp.dot(
                    weights, v_all[head, 0:seen, :], preferred_element_type=f32
                )
                leading[head, rows, :] = jnp.broadcast_to(top, (block, width))

        @pl.when(me == 1)
        def _():
            sent_k.wait_recv()
            split(k_far, 0, kf_all)
            sent_v.wait_recv()
            split(v_far, 2, vf_all)
            for head in range(heads):
                for part in range(2):
                    rows = slice(part * block, (part + 1) * block)
                    scores = lax.dot_general(
                        q_all[head, rows, :],
                        kf_all[head],
                        contract_last,
                        preferred_element_type=f32,
                    )
                    old = leading[head, rows, 0:1]
                    top = jnp.maximum(old, jnp.max(scores, axis=1, keepdims=True))
                    weights = jnp.exp2((scores - top) * scale).astype(bf16)
                    state[head, rows, :] = state[head, rows, :] * jnp.exp2(
                        (old - top) * scale
                    ) + jnp.dot(weights, vf_all[head], preferred_element_type=f32)
            sent_picked.wait_recv()
            picked[...] = picked[...] + picked_far[...]

        for head in range(heads):
            wide[1, pl.ds(head, tok_rows, stride=heads), :] = (
                state[head, :, 0:width] / state[head, :, width:]
            )
        dense_ref[...] = wide[1].astype(bf16)

        loads[6].wait()
        loads[7].wait()
        token = start + lax.broadcasted_iota(jnp.int32, (tok_rows, chosen), 0).astype(f32)
        query = jnp.concatenate([pick(head, qe_in) for head in range(experts)], axis=0)
        logit = jnp.concatenate(
            [
                jnp.sum(
                    one_hot[head].astype(f32) * gate_ref[head : head + 1, :].astype(f32),
                    axis=1,
                    keepdims=True,
                )
                for head in range(experts)
            ],
            axis=0,
        )
        rows = experts * chosen
        scores = lax.dot_general(
            query, picked[0].reshape(rows, width), contract_last, preferred_element_type=f32
        )
        row_rank = lax.broadcasted_iota(jnp.int32, (rows, rows), 0)
        col_rank = lax.broadcasted_iota(jnp.int32, (rows, rows), 1)
        visible = jnp.logical_and(
            col_rank <= row_rank, col_rank // chosen == row_rank // chosen
        )
        scores = jnp.where(visible, scores, NEGATIVE)
        top = jnp.max(scores, axis=1, keepdims=True)
        weights = jnp.where(visible, jnp.exp2((scores - top) * scale), 0.0)
        total = jnp.sum(weights, axis=1, keepdims=True)
        mixed = jnp.dot(
            weights.astype(bf16), picked[1].reshape(rows, width), preferred_element_type=f32
        )
        result = (mixed / (total * (1.0 + jnp.exp(-logit)))).astype(bf16)
        for head in range(experts):
            spread = jnp.where(chosen_rows[head : head + 1, :] == token, 1.0, 0.0).astype(bf16)
            expert_ref[head] = jnp.dot(
                spread,
                result[head * chosen : (head + 1) * chosen],
                preferred_element_type=f32,
            ).astype(bf16)

        @pl.when(first)
        def _():
            sent_k.wait_send()
            sent_v.wait_send()
            sent_picked.wait_send()

    in_hbm = pl.BlockSpec(memory_space=pltpu.HBM)
    in_vmem = pl.BlockSpec(memory_space=pltpu.VMEM)
    flat = (tok_rows * heads, width)
    return pl.pallas_call(
        kernel,
        out_shape=(
            pltpu.VMEM(flat, bf16),
            pltpu.VMEM((experts, tok_rows, width), bf16),
        ),
        in_specs=[in_hbm] * 8,
        out_specs=(in_vmem, in_vmem),
        scratch_shapes=[pltpu.VMEM(flat, bf16)] * 5
        + [pltpu.VMEM((experts, tok_rows, width), bf16)] * 3
        + [
            pltpu.VMEM((3,) + flat, f32),
            pltpu.VMEM((heads, tok_rows, width), bf16),
            pltpu.VMEM((heads, tok_rows, width), bf16),
            pltpu.VMEM((heads, tok_rows, 2 * width), bf16),
            pltpu.VMEM((heads, tok_rows, width), bf16),
            pltpu.VMEM((heads, tok_rows, 2 * width), bf16),
            pltpu.VMEM((heads, tok_rows, 2 * width), f32),
            pltpu.VMEM((heads, tok_rows, width), f32),
            pltpu.VMEM((2, experts, chosen, width), bf16),
            pltpu.VMEM((2, experts, chosen, width), bf16),
            pltpu.VMEM((experts, tok_rows), bf16),
            pltpu.VMEM((experts, chosen), jnp.int32),
            pltpu.SemaphoreType.DMA((8,)),
            pltpu.SemaphoreType.DMA((3,)),
            pltpu.SemaphoreType.DMA((3,)),
        ],
        compiler_params=pltpu.CompilerParams(
            collective_id=0, has_side_effects=True, vmem_limit_bytes=32 * 1024 * 1024
        ),
    )


def write_out(dense, expert):
    def kernel(dense_ref, expert_ref, dense_out, expert_out, sems):
        copies = [
            pltpu.make_async_copy(expert_ref, expert_out, sems.at[0]),
            pltpu.make_async_copy(dense_ref, dense_out, sems.at[1]),
        ]
        for copy in copies:
            copy.start()
        for copy in copies:
            copy.wait()

    return pl.pallas_call(
        kernel,
        out_shape=tuple(
            pltpu.HBM(member.shape, member.dtype) for member in (dense, expert)
        ),
        in_specs=[pl.BlockSpec(memory_space=pltpu.VMEM)] * 2,
        out_specs=tuple([pl.BlockSpec(memory_space=pltpu.HBM)] * 2),
        scratch_shapes=[pltpu.SemaphoreType.DMA((2,))],
    )(dense, expert)


def local_pair(q_dense, k_dense, v_dense, q_expert, k_expert, v_expert, gate_logit, selection):
    tok_rows, heads, width = q_dense.shape
    experts, chosen = selection.shape
    call = nearest_pair(tok_rows, heads, width, experts, chosen)
    dense_out, expert_out = call(
        *(
            pltpu.with_memory_space_constraint(member, pltpu.HBM)
            for member in (
                q_dense.reshape(tok_rows * heads, width),
                k_dense.reshape(tok_rows * heads, width),
                v_dense.reshape(tok_rows * heads, width),
                jnp.transpose(q_expert, (1, 0, 2)),
                jnp.transpose(k_expert, (1, 0, 2)),
                jnp.transpose(v_expert, (1, 0, 2)),
                gate_logit,
                selection,
            )
        )
    )
    dense_out, expert_out = write_out(dense_out, expert_out)
    return (dense_out.reshape(tok_rows, heads, width), jnp.transpose(expert_out, (1, 0, 2)))


def solution(mesh):
    placed = (
        P(("dp", "seq"), "head", None),
        P(("dp", "seq"), "head", None),
        P(("dp", "seq"), "head", None),
        P(("dp", "seq"), "head", None),
        P(("dp", "seq"), "head", None),
        P(("dp", "seq"), "head", None),
        P("head", ("dp", "seq")),
        P("head", "dp"),
    )
    return jax.shard_map(
        local_pair if mesh.shape["seq"] == 2 else local,
        mesh=mesh,
        in_specs=placed,
        out_specs=(P(("dp", "seq"), "head", None), P(("dp", "seq"), "head", None)),
        check_vma=False,
    )
```

```python
import math

import jax
import jax.numpy as jnp
from jax import lax
from jax.experimental import pallas as pl
from jax.experimental.pallas import tpu as pltpu
from jax.sharding import PartitionSpec as P

NEGATIVE = -1e30


def plain_rows(rows, tok_rows, count):
    return rows


def online_update(state, queries, query_pos, keys, values, key_pos, scale):
    leading, total, summed = state
    scores = jnp.einsum("qhd,khd->qhk", queries, keys, preferred_element_type=jnp.float32) * scale
    visible = key_pos[None, None, :] <= query_pos[:, None, None]
    scores = jnp.where(visible, scores, NEGATIVE)
    new_leading = jnp.maximum(leading, jnp.max(scores, axis=2))
    shrink = jnp.exp(leading - new_leading)
    weights = jnp.where(visible, jnp.exp(scores - new_leading[:, :, None]), 0.0)
    total = total * shrink + jnp.sum(weights, axis=2)
    moved = jnp.einsum(
        "qhk,khd->qhd", weights.astype(jnp.bfloat16), values, preferred_element_type=jnp.float32
    )
    return (new_leading, total, summed * shrink[:, :, None] + moved)


def dense_heads(queries, keys, values, position_map):
    tok_rows, heads, width = queries.shape
    count = lax.axis_size("seq")
    half_rows = tok_rows // 2
    own_rows = lax.axis_index("seq") * tok_rows + jnp.arange(tok_rows, dtype=jnp.int32)
    query_pos = position_map(own_rows, tok_rows, count).reshape(2, half_rows)
    groups = queries.reshape(2, half_rows, heads, width)
    scale = 1.0 / math.sqrt(width)
    blank = (
        jnp.full((half_rows, heads), NEGATIVE, jnp.float32),
        jnp.zeros((half_rows, heads), jnp.float32),
        jnp.zeros((half_rows, heads, width), jnp.float32),
    )
    key_rows = lax.all_gather(keys, "seq", axis=0, tiled=True)
    value_rows = lax.all_gather(values, "seq", axis=0, tiled=True)
    length = key_rows.shape[0]
    block = math.gcd(length, 512)
    count_blocks = length // block
    key_pos = position_map(jnp.arange(length, dtype=jnp.int32), tok_rows, count).reshape(
        count_blocks, block
    )
    key_blocks = key_rows.reshape(count_blocks, block, heads, width)
    value_blocks = value_rows.reshape(count_blocks, block, heads, width)

    def advance(state, item):
        key_block, value_block, block_pos = item
        result = []
        for group in range(2):
            seen = jnp.min(block_pos) <= jnp.max(query_pos[group])
            result.append(
                lax.cond(
                    seen,
                    lambda inner, member=group: online_update(
                        inner,
                        groups[member],
                        query_pos[member],
                        key_block,
                        value_block,
                        block_pos,
                        scale,
                    ),
                    lambda inner: inner,
                    state[group],
                )
            )
        return (tuple(result), None)

    final_state, unused = lax.scan(advance, (blank, blank), (key_blocks, value_blocks, key_pos))
    outputs = [
        (summed / total[:, :, None]).astype(jnp.bfloat16) for leading, total, summed in final_state
    ]
    return jnp.concatenate(outputs, axis=0)


def attend_ranked(query_rows, query_ranks, keys, values, gate_rows):
    heads, rows, width = query_rows.shape
    block = math.gcd(rows, 512)
    scale = 1.0 / math.sqrt(width)
    key_ranks = jnp.arange(keys.shape[1], dtype=jnp.int32)

    def one_block(index):
        scores = (
            jnp.einsum("erd,ekd->erk", query_rows, keys, preferred_element_type=jnp.float32) * scale
        )
        visible = key_ranks[None, None, :] <= query_ranks[:, :, None]
        scores = jnp.where(visible, scores, NEGATIVE)
        leading = jnp.max(scores, axis=2, keepdims=True)
        weights = jnp.where(visible, jnp.exp(scores - leading), 0.0)
        total = jnp.sum(weights, axis=2, keepdims=True)
        mixed = (
            jnp.einsum(
                "erk,ekd->erd",
                weights.astype(jnp.bfloat16),
                values,
                preferred_element_type=jnp.float32,
            )
            / total
        )
        return (mixed * jax.nn.sigmoid(gate_rows.astype(jnp.float32))[:, :, None]).astype(
            jnp.bfloat16
        )

    blocks = lax.map(one_block, jnp.arange(rows // block, dtype=jnp.int32))
    return jnp.moveaxis(blocks, 0, 1).reshape(heads, rows, width)


def sparse_heads(queries, keys, values, gate_logit, selection):
    tok_rows, heads, width = queries.shape
    chosen = selection.shape[1]
    start = lax.axis_index("seq") * tok_rows
    positions = start + jnp.arange(tok_rows, dtype=jnp.int32)
    matches = selection[:, :, None] == positions[None, None, :]
    one_hot = matches.astype(jnp.bfloat16)

    def pick(source):
        return jnp.einsum(
            "ent,ted->end", one_hot, source, preferred_element_type=jnp.float32
        ).astype(jnp.bfloat16)

    gate_rows = jnp.einsum("ent,et->en", one_hot, gate_logit, preferred_element_type=jnp.float32)
    gathered = (
        lax.psum(pick(queries), "seq").astype(jnp.float32),
        lax.psum(pick(keys), "seq").astype(jnp.float32),
        lax.psum(pick(values), "seq").astype(jnp.float32),
        lax.psum(gate_rows.astype(jnp.bfloat16), "seq").astype(jnp.float32),
    )
    picked_q, picked_k, picked_v, picked_gate = [member.astype(jnp.bfloat16) for member in gathered]
    all_ranks = jnp.broadcast_to(jnp.arange(chosen, dtype=jnp.int32)[None, :], (heads, chosen))
    results = attend_ranked(picked_q, all_ranks, picked_k, picked_v, picked_gate)
    return jnp.einsum("ent,end->ted", one_hot, results, preferred_element_type=jnp.float32).astype(
        jnp.bfloat16
    )


def local(q_dense, k_dense, v_dense, q_expert, k_expert, v_expert, gate_logit, selection):
    dense_out = dense_heads(q_dense, k_dense, v_dense, plain_rows)
    expert_out = sparse_heads(q_expert, k_expert, v_expert, gate_logit, selection)
    return (dense_out, expert_out)

def nearest_pair(tok_rows, heads, width, experts, chosen):
    scale = math.log2(math.e) / math.sqrt(width)
    block = tok_rows // 2
    contract_last = (((1,), (1,)), ((), ()))
    f32, bf16 = jnp.float32, jnp.bfloat16

    def kernel(
        q_ref, k_ref, v_ref, qe_ref, ke_ref, ve_ref, gate_hbm, sel_hbm,
        dense_ref, expert_ref,
        q_in, k_in, v_in, qe_in, ke_in, ve_in,
        wide, q_all, k_all, v_all, kf_all, vf_all, state, leading,
        picked, picked_far, gate_ref, sel_ref, in_sem, send_sem, recv_sem,
    ):
        me = lax.axis_index("seq")
        first = me == 0
        barrier = pltpu.get_barrier_semaphore()
        partner = {"seq": 1 - me}

        def far_copy(number, source, target):
            return pltpu.make_async_remote_copy(
                src_ref=source,
                dst_ref=target,
                send_sem=send_sem.at[number],
                recv_sem=recv_sem.at[number],
                device_id=partner,
                device_id_type=pl.DeviceIdType.MESH,
            )

        sent_k = far_copy(0, k_all, kf_all)
        sent_v = far_copy(1, v_all.at[:, :, 0:width], vf_all.at[:, :, 0:width])
        sent_picked = far_copy(2, picked, picked_far)

        @pl.when(me == 1)
        def _():
            pl.semaphore_signal(
                barrier, inc=1, device_id=partner, device_id_type=pl.DeviceIdType.MESH
            )

        loads = [
            pltpu.make_async_copy(source, target, in_sem.at[number])
            for number, (source, target) in enumerate(
                (
                    (k_ref, k_in),
                    (v_ref, v_in),
                    (sel_hbm, sel_ref),
                    (ke_ref, ke_in),
                    (ve_ref, ve_in),
                    (q_ref, q_in),
                    (qe_ref, qe_in),
                    (gate_hbm, gate_ref),
                )
            )
        ]
        for load in loads:
            load.start()

        def split(source, number, target):
            wide[number] = source[...].astype(f32)
            for head in range(heads):
                target[head, :, 0:width] = wide[
                    number, pl.ds(head, tok_rows, stride=heads), :
                ].astype(bf16)

        ones = jnp.ones((tok_rows, width), bf16)
        for head in range(heads):
            v_all[head, :, width:] = ones
            vf_all[head, :, width:] = ones
        loads[0].wait()
        split(k_in, 0, k_all)

        @pl.when(first)
        def _():
            pl.semaphore_wait(barrier, 1)
            sent_k.start()

        loads[1].wait()
        split(v_in, 2, v_all)

        @pl.when(first)
        def _():
            sent_v.start()

        loads[2].wait()
        chosen_rows = sel_ref[...].astype(f32)
        start = (me * tok_rows).astype(f32)
        places = start + lax.broadcasted_iota(jnp.int32, (chosen, tok_rows), 1).astype(f32)
        one_hot = []
        for head in range(experts):
            square = jnp.broadcast_to(chosen_rows[head : head + 1, :], (chosen, chosen)).T
            one_hot.append(
                jnp.where(square[:, 0:1] == places, 1.0, 0.0).astype(bf16)
            )

        def pick(head, source):
            return jnp.dot(one_hot[head], source[head], preferred_element_type=f32).astype(bf16)

        loads[3].wait()
        for head in range(experts):
            picked[0, head] = pick(head, ke_in)
        loads[4].wait()
        for head in range(experts):
            picked[1, head] = pick(head, ve_in)

        @pl.when(first)
        def _():
            sent_picked.start()

        loads[5].wait()
        split(q_in, 1, q_all)

        for head in range(heads):
            for part in range(2):
                rows = slice(part * block, (part + 1) * block)
                seen = (part + 1) * block
                scores = lax.dot_general(
                    q_all[head, rows, :],
                    k_all[head, 0:seen, :],
                    contract_last,
                    preferred_element_type=f32,
                )
                row_pos = part * block + lax.broadcasted_iota(jnp.int32, (block, seen), 0)
                col_pos = lax.broadcasted_iota(jnp.int32, (block, seen), 1)
                scores = jnp.where(col_pos <= row_pos, scores, NEGATIVE)
                top = jnp.max(scores, axis=1, keepdims=True)
                weights = jnp.exp2((scores - top) * scale).astype(bf16)
                state[head, rows, :] = jnp.dot(
                    weights, v_all[head, 0:seen, :], preferred_element_type=f32
                )
                leading[head, rows, :] = jnp.broadcast_to(top, (block, width))

        @pl.when(me == 1)
        def _():
            sent_k.wait_recv()
            for head in range(heads):
                for part in range(2):
                    rows = slice(part * block, (part + 1) * block)
                    scores = lax.dot_general(
                        q_all[head, rows, :],
                        kf_all[head],
                        contract_last,
                        preferred_element_type=f32,
                    )
                    old = leading[head, rows, :]
                    top = jnp.maximum(old, jnp.max(scores, axis=1, keepdims=True))
                    weights = jnp.concatenate(
                        [
                            jnp.exp2((scores[:, left : left + width] - top) * scale)
                            for left in range(0, tok_rows, width)
                        ],
                        axis=1,
                    ).astype(bf16)
                    if head == 0 and part == 0:
                        sent_v.wait_recv()
                    shrink = jnp.exp2((old - top) * scale)
                    state[head, rows, :] = state[head, rows, :] * jnp.concatenate(
                        [shrink, shrink], axis=1
                    ) + jnp.dot(weights, vf_all[head], preferred_element_type=f32)
            sent_picked.wait_recv()
            picked[...] = picked[...] + picked_far[...]

        for head in range(heads):
            wide[1, pl.ds(head, tok_rows, stride=heads), :] = (
                state[head, :, 0:width] / state[head, :, width:]
            )
        dense_ref[...] = wide[1].astype(bf16)

        loads[6].wait()
        loads[7].wait()
        token = start + lax.broadcasted_iota(jnp.int32, (tok_rows, chosen), 0).astype(f32)
        query = jnp.concatenate([pick(head, qe_in) for head in range(experts)], axis=0)
        logit = jnp.concatenate(
            [
                jnp.sum(
                    one_hot[head].astype(f32) * gate_ref[head : head + 1, :].astype(f32),
                    axis=1,
                    keepdims=True,
                )
                for head in range(experts)
            ],
            axis=0,
        )
        rows = experts * chosen
        scores = lax.dot_general(
            query, picked[0].reshape(rows, width), contract_last, preferred_element_type=f32
        )
        row_rank = lax.broadcasted_iota(jnp.int32, (rows, rows), 0)
        col_rank = lax.broadcasted_iota(jnp.int32, (rows, rows), 1)
        visible = jnp.logical_and(
            col_rank <= row_rank, col_rank // chosen == row_rank // chosen
        )
        scores = jnp.where(visible, scores, NEGATIVE)
        top = jnp.max(scores, axis=1, keepdims=True)
        weights = jnp.where(visible, jnp.exp2((scores - top) * scale), 0.0)
        total = jnp.sum(weights, axis=1, keepdims=True)
        mixed = jnp.dot(
            weights.astype(bf16), picked[1].reshape(rows, width), preferred_element_type=f32
        )
        result = (mixed / (total * (1.0 + jnp.exp(-logit)))).astype(bf16)
        for head in range(experts):
            spread = jnp.where(chosen_rows[head : head + 1, :] == token, 1.0, 0.0).astype(bf16)
            expert_ref[head] = jnp.dot(
                spread,
                result[head * chosen : (head + 1) * chosen],
                preferred_element_type=f32,
            ).astype(bf16)

        @pl.when(first)
        def _():
            sent_k.wait_send()
            sent_v.wait_send()
            sent_picked.wait_send()

    in_hbm = pl.BlockSpec(memory_space=pltpu.HBM)
    in_vmem = pl.BlockSpec(memory_space=pltpu.VMEM)
    flat = (tok_rows * heads, width)
    return pl.pallas_call(
        kernel,
        out_shape=(
            pltpu.VMEM(flat, bf16),
            pltpu.VMEM((experts, tok_rows, width), bf16),
        ),
        in_specs=[in_hbm] * 8,
        out_specs=(in_vmem, in_vmem),
        scratch_shapes=[pltpu.VMEM(flat, bf16)] * 3
        + [pltpu.VMEM((experts, tok_rows, width), bf16)] * 3
        + [
            pltpu.VMEM((3,) + flat, f32),
            pltpu.VMEM((heads, tok_rows, width), bf16),
            pltpu.VMEM((heads, tok_rows, width), bf16),
            pltpu.VMEM((heads, tok_rows, 2 * width), bf16),
            pltpu.VMEM((heads, tok_rows, width), bf16),
            pltpu.VMEM((heads, tok_rows, 2 * width), bf16),
            pltpu.VMEM((heads, tok_rows, 2 * width), f32),
            pltpu.VMEM((heads, tok_rows, width), f32),
            pltpu.VMEM((2, experts, chosen, width), bf16),
            pltpu.VMEM((2, experts, chosen, width), bf16),
            pltpu.VMEM((experts, tok_rows), bf16),
            pltpu.VMEM((experts, chosen), jnp.int32),
            pltpu.SemaphoreType.DMA((8,)),
            pltpu.SemaphoreType.DMA((3,)),
            pltpu.SemaphoreType.DMA((3,)),
        ],
        compiler_params=pltpu.CompilerParams(
            collective_id=0, has_side_effects=True, vmem_limit_bytes=32 * 1024 * 1024
        ),
    )


def write_out(dense, expert):
    def kernel(dense_ref, expert_ref, dense_out, expert_out, sems):
        copies = [
            pltpu.make_async_copy(expert_ref, expert_out, sems.at[0]),
            pltpu.make_async_copy(dense_ref, dense_out, sems.at[1]),
        ]
        for copy in copies:
            copy.start()
        for copy in copies:
            copy.wait()

    return pl.pallas_call(
        kernel,
        out_shape=tuple(
            pltpu.HBM(member.shape, member.dtype) for member in (dense, expert)
        ),
        in_specs=[pl.BlockSpec(memory_space=pltpu.VMEM)] * 2,
        out_specs=tuple([pl.BlockSpec(memory_space=pltpu.HBM)] * 2),
        scratch_shapes=[pltpu.SemaphoreType.DMA((2,))],
        compiler_params=pltpu.CompilerParams(vmem_limit_bytes=4 * 1024 * 1024),
    )(
        pltpu.with_memory_space_constraint(dense, pltpu.VMEM),
        pltpu.with_memory_space_constraint(expert, pltpu.VMEM),
    )


def local_pair(q_dense, k_dense, v_dense, q_expert, k_expert, v_expert, gate_logit, selection):
    tok_rows, heads, width = q_dense.shape
    experts, chosen = selection.shape
    call = nearest_pair(tok_rows, heads, width, experts, chosen)
    dense_out, expert_out = call(
        *(
            pltpu.with_memory_space_constraint(member, pltpu.HBM)
            for member in (
                q_dense.reshape(tok_rows * heads, width),
                k_dense.reshape(tok_rows * heads, width),
                v_dense.reshape(tok_rows * heads, width),
                jnp.transpose(q_expert, (1, 0, 2)),
                jnp.transpose(k_expert, (1, 0, 2)),
                jnp.transpose(v_expert, (1, 0, 2)),
                gate_logit,
                selection,
            )
        )
    )
    dense_out, expert_out = write_out(dense_out, expert_out)
    return (dense_out.reshape(tok_rows, heads, width), jnp.transpose(expert_out, (1, 0, 2)))


def solution(mesh):
    placed = (
        P(("dp", "seq"), "head", None),
        P(("dp", "seq"), "head", None),
        P(("dp", "seq"), "head", None),
        P(("dp", "seq"), "head", None),
        P(("dp", "seq"), "head", None),
        P(("dp", "seq"), "head", None),
        P("head", ("dp", "seq")),
        P("head", "dp"),
    )
    return jax.shard_map(
        local_pair if mesh.shape["seq"] == 2 else local,
        mesh=mesh,
        in_specs=placed,
        out_specs=(P(("dp", "seq"), "head", None), P(("dp", "seq"), "head", None)),
        check_vma=False,
    )
```

```python
import math

import jax
import jax.numpy as jnp
from jax import lax
from jax.experimental import pallas as pl
from jax.experimental.pallas import tpu as pltpu
from jax.sharding import PartitionSpec as P

NEGATIVE = -1e30


def plain_rows(rows, tok_rows, count):
    return rows


def online_update(state, queries, query_pos, keys, values, key_pos, scale):
    leading, total, summed = state
    scores = jnp.einsum("qhd,khd->qhk", queries, keys, preferred_element_type=jnp.float32) * scale
    visible = key_pos[None, None, :] <= query_pos[:, None, None]
    scores = jnp.where(visible, scores, NEGATIVE)
    new_leading = jnp.maximum(leading, jnp.max(scores, axis=2))
    shrink = jnp.exp(leading - new_leading)
    weights = jnp.where(visible, jnp.exp(scores - new_leading[:, :, None]), 0.0)
    total = total * shrink + jnp.sum(weights, axis=2)
    moved = jnp.einsum(
        "qhk,khd->qhd", weights.astype(jnp.bfloat16), values, preferred_element_type=jnp.float32
    )
    return (new_leading, total, summed * shrink[:, :, None] + moved)


def dense_heads(queries, keys, values, position_map):
    tok_rows, heads, width = queries.shape
    count = lax.axis_size("seq")
    half_rows = tok_rows // 2
    own_rows = lax.axis_index("seq") * tok_rows + jnp.arange(tok_rows, dtype=jnp.int32)
    query_pos = position_map(own_rows, tok_rows, count).reshape(2, half_rows)
    groups = queries.reshape(2, half_rows, heads, width)
    scale = 1.0 / math.sqrt(width)
    blank = (
        jnp.full((half_rows, heads), NEGATIVE, jnp.float32),
        jnp.zeros((half_rows, heads), jnp.float32),
        jnp.zeros((half_rows, heads, width), jnp.float32),
    )
    key_rows = lax.all_gather(keys, "seq", axis=0, tiled=True)
    value_rows = lax.all_gather(values, "seq", axis=0, tiled=True)
    length = key_rows.shape[0]
    block = math.gcd(length, 512)
    count_blocks = length // block
    key_pos = position_map(jnp.arange(length, dtype=jnp.int32), tok_rows, count).reshape(
        count_blocks, block
    )
    key_blocks = key_rows.reshape(count_blocks, block, heads, width)
    value_blocks = value_rows.reshape(count_blocks, block, heads, width)

    def advance(state, item):
        key_block, value_block, block_pos = item
        result = []
        for group in range(2):
            seen = jnp.min(block_pos) <= jnp.max(query_pos[group])
            result.append(
                lax.cond(
                    seen,
                    lambda inner, member=group: online_update(
                        inner,
                        groups[member],
                        query_pos[member],
                        key_block,
                        value_block,
                        block_pos,
                        scale,
                    ),
                    lambda inner: inner,
                    state[group],
                )
            )
        return (tuple(result), None)

    final_state, unused = lax.scan(advance, (blank, blank), (key_blocks, value_blocks, key_pos))
    outputs = [
        (summed / total[:, :, None]).astype(jnp.bfloat16) for leading, total, summed in final_state
    ]
    return jnp.concatenate(outputs, axis=0)


def attend_ranked(query_rows, query_ranks, keys, values, gate_rows):
    heads, rows, width = query_rows.shape
    block = math.gcd(rows, 512)
    scale = 1.0 / math.sqrt(width)
    key_ranks = jnp.arange(keys.shape[1], dtype=jnp.int32)

    def one_block(index):
        scores = (
            jnp.einsum("erd,ekd->erk", query_rows, keys, preferred_element_type=jnp.float32) * scale
        )
        visible = key_ranks[None, None, :] <= query_ranks[:, :, None]
        scores = jnp.where(visible, scores, NEGATIVE)
        leading = jnp.max(scores, axis=2, keepdims=True)
        weights = jnp.where(visible, jnp.exp(scores - leading), 0.0)
        total = jnp.sum(weights, axis=2, keepdims=True)
        mixed = (
            jnp.einsum(
                "erk,ekd->erd",
                weights.astype(jnp.bfloat16),
                values,
                preferred_element_type=jnp.float32,
            )
            / total
        )
        return (mixed * jax.nn.sigmoid(gate_rows.astype(jnp.float32))[:, :, None]).astype(
            jnp.bfloat16
        )

    blocks = lax.map(one_block, jnp.arange(rows // block, dtype=jnp.int32))
    return jnp.moveaxis(blocks, 0, 1).reshape(heads, rows, width)


def sparse_heads(queries, keys, values, gate_logit, selection):
    tok_rows, heads, width = queries.shape
    chosen = selection.shape[1]
    start = lax.axis_index("seq") * tok_rows
    positions = start + jnp.arange(tok_rows, dtype=jnp.int32)
    matches = selection[:, :, None] == positions[None, None, :]
    one_hot = matches.astype(jnp.bfloat16)

    def pick(source):
        return jnp.einsum(
            "ent,ted->end", one_hot, source, preferred_element_type=jnp.float32
        ).astype(jnp.bfloat16)

    gate_rows = jnp.einsum("ent,et->en", one_hot, gate_logit, preferred_element_type=jnp.float32)
    gathered = (
        lax.psum(pick(queries), "seq").astype(jnp.float32),
        lax.psum(pick(keys), "seq").astype(jnp.float32),
        lax.psum(pick(values), "seq").astype(jnp.float32),
        lax.psum(gate_rows.astype(jnp.bfloat16), "seq").astype(jnp.float32),
    )
    picked_q, picked_k, picked_v, picked_gate = [member.astype(jnp.bfloat16) for member in gathered]
    all_ranks = jnp.broadcast_to(jnp.arange(chosen, dtype=jnp.int32)[None, :], (heads, chosen))
    results = attend_ranked(picked_q, all_ranks, picked_k, picked_v, picked_gate)
    return jnp.einsum("ent,end->ted", one_hot, results, preferred_element_type=jnp.float32).astype(
        jnp.bfloat16
    )


def local(q_dense, k_dense, v_dense, q_expert, k_expert, v_expert, gate_logit, selection):
    dense_out = dense_heads(q_dense, k_dense, v_dense, plain_rows)
    expert_out = sparse_heads(q_expert, k_expert, v_expert, gate_logit, selection)
    return (dense_out, expert_out)

def nearest_pair(tok_rows, heads, width, experts, chosen):
    scale = math.log2(math.e) / math.sqrt(width)
    block = tok_rows // 2
    picks = experts * chosen
    contract_last = (((1,), (1,)), ((), ()))
    f32, bf16 = jnp.float32, jnp.bfloat16

    def kernel(
        q_ref, k_ref, v_ref, qe_ref, ke_ref, ve_ref, gate_hbm, sel_hbm,
        dense_ref, expert_ref,
        q_in, k_in, v_in, qe_in, ke_in, ve_in,
        wide, q_all, k_all, v_all, kf_all, vf_all, state, leading,
        picked, picked_far, gate_ref, sel_ref, in_sem, send_sem, recv_sem,
    ):
        me = lax.axis_index("seq")
        first = me == 0
        barrier = pltpu.get_barrier_semaphore()
        partner = {"seq": 1 - me}

        def far_copy(number, source, target):
            return pltpu.make_async_remote_copy(
                src_ref=source,
                dst_ref=target,
                send_sem=send_sem.at[number],
                recv_sem=recv_sem.at[number],
                device_id=partner,
                device_id_type=pl.DeviceIdType.MESH,
            )

        sent_k = far_copy(0, k_all, kf_all)
        sent_v = far_copy(1, v_all.at[:, :, 0:width], vf_all.at[:, :, 0:width])
        sent_picked = far_copy(2, picked, picked_far)

        @pl.when(me == 1)
        def _():
            pl.semaphore_signal(
                barrier, inc=1, device_id=partner, device_id_type=pl.DeviceIdType.MESH
            )

        loads = [
            pltpu.make_async_copy(source, target, in_sem.at[number])
            for number, (source, target) in enumerate(
                (
                    (k_ref, k_in),
                    (v_ref, v_in),
                    (sel_hbm, sel_ref),
                    (ke_ref, ke_in),
                    (ve_ref, ve_in),
                    (q_ref, q_in),
                    (qe_ref, qe_in),
                    (gate_hbm, gate_ref),
                )
            )
        ]
        for load in loads:
            load.start()

        def split(source, number, target):
            wide[number] = source[...].astype(f32)
            for head in range(heads):
                target[head, :, 0:width] = wide[
                    number, pl.ds(head, tok_rows, stride=heads), :
                ].astype(bf16)

        ones = jnp.ones((tok_rows, width), bf16)
        for head in range(heads):
            v_all[head, :, width:] = ones
            vf_all[head, :, width:] = ones
        for number in range(5):
            loads[number].wait()
        chosen_rows = sel_ref[...].astype(f32)
        start = (me * tok_rows).astype(f32)
        places = start + lax.broadcasted_iota(jnp.int32, (chosen, tok_rows), 1).astype(f32)
        one_hot = []
        for head in range(experts):
            square = jnp.broadcast_to(chosen_rows[head : head + 1, :], (chosen, chosen)).T
            one_hot.append(
                jnp.where(square[:, 0:1] == places, 1.0, 0.0).astype(bf16)
            )
        split(k_in, 0, k_all)
        for head in range(experts):
            both = jnp.concatenate([ke_in[head], ve_in[head]], axis=1)
            picked[head * chosen : (head + 1) * chosen, :] = jnp.dot(
                one_hot[head], both, preferred_element_type=f32
            ).astype(bf16)
        split(v_in, 2, v_all)

        @pl.when(first)
        def _():
            pl.semaphore_wait(barrier, 1)
            sent_k.start()
            sent_v.start()
            sent_picked.start()

        for number in range(5, 8):
            loads[number].wait()
        split(q_in, 1, q_all)

        def local_scores(head, part):
            rows = slice(part * block, (part + 1) * block)
            scores = lax.dot_general(
                q_all[head, rows, :],
                k_all[head, 0 : (part + 1) * block, :],
                contract_last,
                preferred_element_type=f32,
            )
            edge = scores[:, part * block :]
            lower = lax.broadcasted_iota(jnp.int32, (block, block), 1) <= (
                lax.broadcasted_iota(jnp.int32, (block, block), 0)
            )
            edge = jnp.where(lower, edge, NEGATIVE)
            return edge if part == 0 else jnp.concatenate([scores[:, : part * block], edge], axis=1)

        def local_mix(head, part, scores):
            top = jnp.max(scores, axis=1, keepdims=True)
            weights = jnp.exp2((scores - top) * scale).astype(bf16)
            return top, jnp.dot(
                weights, v_all[head, 0 : (part + 1) * block, :], preferred_element_type=f32
            )

        def far_scores(head, part):
            return lax.dot_general(
                q_all[head, part * block : (part + 1) * block, :],
                kf_all[head],
                contract_last,
                preferred_element_type=f32,
            )

        def far_mix(head, part, scores):
            rows = slice(part * block, (part + 1) * block)
            old = leading[head, rows, :]
            top = jnp.maximum(old, jnp.max(scores, axis=1, keepdims=True))
            weights = jnp.concatenate(
                [
                    jnp.exp2((scores[:, left : left + width] - top) * scale)
                    for left in range(0, tok_rows, width)
                ],
                axis=1,
            ).astype(bf16)
            shrink = jnp.exp2((old - top) * scale)
            return state[head, rows, :] * jnp.concatenate([shrink, shrink], axis=1) + jnp.dot(
                weights, vf_all[head], preferred_element_type=f32
            )

        def finish(head, part, mixed):
            wide[1, pl.ds(part * block * heads + head, block, stride=heads), :] = (
                mixed[:, 0:width] / mixed[:, width:]
            )

        def keep(head, part, top, mixed):
            rows = slice(part * block, (part + 1) * block)
            state[head, rows, :] = mixed
            leading[head, rows, :] = jnp.broadcast_to(top, (block, width))

        pieces = [(head, part) for head in range(heads) for part in range(2)]

        def staged(score, use):
            ready = [score(*pieces[0]), score(*pieces[1])]
            for number, piece in enumerate(pieces):
                if number + 2 < len(pieces):
                    ready.append(score(*pieces[number + 2]))
                use(*piece, ready[number])

        def expert_query():
            query = jnp.concatenate(
                [
                    jnp.dot(one_hot[head], qe_in[head], preferred_element_type=f32)
                    for head in range(experts)
                ],
                axis=0,
            ).astype(bf16)
            logit = jnp.concatenate(
                [
                    jnp.sum(
                        one_hot[head].astype(f32) * gate_ref[head : head + 1, :].astype(f32),
                        axis=1,
                        keepdims=True,
                    )
                    for head in range(experts)
                ],
                axis=0,
            )
            return query, 1.0 + jnp.exp(-logit)

        def expert_result(query, gate, pairs):
            scores = lax.dot_general(
                query, pairs[:, 0:width], contract_last, preferred_element_type=f32
            )
            row_rank = lax.broadcasted_iota(jnp.int32, (picks, picks), 0)
            col_rank = lax.broadcasted_iota(jnp.int32, (picks, picks), 1)
            visible = jnp.logical_and(
                col_rank <= row_rank, col_rank // chosen == row_rank // chosen
            )
            scores = jnp.where(visible, scores, NEGATIVE)
            top = jnp.max(scores, axis=1, keepdims=True)
            weights = jnp.where(visible, jnp.exp2((scores - top) * scale), 0.0)
            total = jnp.sum(weights, axis=1, keepdims=True)
            mixed = jnp.dot(
                weights.astype(bf16), pairs[:, width:], preferred_element_type=f32
            )
            return (mixed / (total * gate)).astype(bf16)

        def expert_write(result):
            token = start + lax.broadcasted_iota(jnp.int32, (tok_rows, chosen), 0).astype(f32)
            for head in range(experts):
                spread = jnp.where(
                    chosen_rows[head : head + 1, :] == token, 1.0, 0.0
                ).astype(bf16)
                expert_ref[head] = jnp.dot(
                    spread,
                    result[head * chosen : (head + 1) * chosen],
                    preferred_element_type=f32,
                ).astype(bf16)

        @pl.when(first)
        def _():
            result = expert_result(*expert_query(), picked[...])
            staged(
                local_scores,
                lambda head, part, scores: finish(head, part, local_mix(head, part, scores)[1]),
            )
            expert_write(result)
            dense_ref[...] = wide[1].astype(bf16)

        @pl.when(me == 1)
        def _():
            query, gate = expert_query()
            staged(
                local_scores,
                lambda head, part, scores: keep(head, part, *local_mix(head, part, scores)),
            )
            sent_k.wait_recv()
            sent_v.wait_recv()
            sent_picked.wait_recv()
            result = expert_result(query, gate, picked[...] + picked_far[...])
            staged(
                far_scores,
                lambda head, part, scores: finish(head, part, far_mix(head, part, scores)),
            )
            expert_write(result)
            dense_ref[...] = wide[1].astype(bf16)

        @pl.when(first)
        def _():
            sent_k.wait_send()
            sent_v.wait_send()
            sent_picked.wait_send()

    in_hbm = pl.BlockSpec(memory_space=pltpu.HBM)
    in_vmem = pl.BlockSpec(memory_space=pltpu.VMEM)
    flat = (tok_rows * heads, width)
    return pl.pallas_call(
        kernel,
        out_shape=(
            pltpu.VMEM(flat, bf16),
            pltpu.VMEM((experts, tok_rows, width), bf16),
        ),
        in_specs=[in_hbm] * 8,
        out_specs=(in_vmem, in_vmem),
        scratch_shapes=[pltpu.VMEM(flat, bf16)] * 3
        + [pltpu.VMEM((experts, tok_rows, width), bf16)] * 3
        + [
            pltpu.VMEM((3,) + flat, f32),
            pltpu.VMEM((heads, tok_rows, width), bf16),
            pltpu.VMEM((heads, tok_rows, width), bf16),
            pltpu.VMEM((heads, tok_rows, 2 * width), bf16),
            pltpu.VMEM((heads, tok_rows, width), bf16),
            pltpu.VMEM((heads, tok_rows, 2 * width), bf16),
            pltpu.VMEM((heads, tok_rows, 2 * width), f32),
            pltpu.VMEM((heads, tok_rows, width), f32),
            pltpu.VMEM((picks, 2 * width), bf16),
            pltpu.VMEM((picks, 2 * width), bf16),
            pltpu.VMEM((experts, tok_rows), bf16),
            pltpu.VMEM((experts, chosen), jnp.int32),
            pltpu.SemaphoreType.DMA((8,)),
            pltpu.SemaphoreType.DMA((3,)),
            pltpu.SemaphoreType.DMA((3,)),
        ],
        compiler_params=pltpu.CompilerParams(
            collective_id=0, has_side_effects=True, vmem_limit_bytes=32 * 1024 * 1024
        ),
    )


def write_out(dense, expert):
    def kernel(dense_ref, expert_ref, dense_out, expert_out, sems):
        copies = [
            pltpu.make_async_copy(expert_ref, expert_out, sems.at[0]),
            pltpu.make_async_copy(dense_ref, dense_out, sems.at[1]),
        ]
        for copy in copies:
            copy.start()
        for copy in copies:
            copy.wait()

    return pl.pallas_call(
        kernel,
        out_shape=tuple(
            pltpu.HBM(member.shape, member.dtype) for member in (dense, expert)
        ),
        in_specs=[pl.BlockSpec(memory_space=pltpu.VMEM)] * 2,
        out_specs=tuple([pl.BlockSpec(memory_space=pltpu.HBM)] * 2),
        scratch_shapes=[pltpu.SemaphoreType.DMA((2,))],
        compiler_params=pltpu.CompilerParams(vmem_limit_bytes=4 * 1024 * 1024),
    )(
        pltpu.with_memory_space_constraint(dense, pltpu.VMEM),
        pltpu.with_memory_space_constraint(expert, pltpu.VMEM),
    )


def local_pair(q_dense, k_dense, v_dense, q_expert, k_expert, v_expert, gate_logit, selection):
    tok_rows, heads, width = q_dense.shape
    experts, chosen = selection.shape
    call = nearest_pair(tok_rows, heads, width, experts, chosen)
    dense_out, expert_out = call(
        *(
            pltpu.with_memory_space_constraint(member, pltpu.HBM)
            for member in (
                q_dense.reshape(tok_rows * heads, width),
                k_dense.reshape(tok_rows * heads, width),
                v_dense.reshape(tok_rows * heads, width),
                jnp.transpose(q_expert, (1, 0, 2)),
                jnp.transpose(k_expert, (1, 0, 2)),
                jnp.transpose(v_expert, (1, 0, 2)),
                gate_logit,
                selection,
            )
        )
    )
    dense_out, expert_out = write_out(dense_out, expert_out)
    return (dense_out.reshape(tok_rows, heads, width), jnp.transpose(expert_out, (1, 0, 2)))


def solution(mesh):
    placed = (
        P(("dp", "seq"), "head", None),
        P(("dp", "seq"), "head", None),
        P(("dp", "seq"), "head", None),
        P(("dp", "seq"), "head", None),
        P(("dp", "seq"), "head", None),
        P(("dp", "seq"), "head", None),
        P("head", ("dp", "seq")),
        P("head", "dp"),
    )
    return jax.shard_map(
        local_pair if mesh.shape["seq"] == 2 else local,
        mesh=mesh,
        in_specs=placed,
        out_specs=(P(("dp", "seq"), "head", None), P(("dp", "seq"), "head", None)),
        check_vma=False,
    )
```

```python
import math

import jax
import jax.numpy as jnp
from jax import lax
from jax.experimental import pallas as pl
from jax.experimental.pallas import tpu as pltpu
from jax.sharding import PartitionSpec as P

NEGATIVE = -1e30


def plain_rows(rows, tok_rows, count):
    return rows


def online_update(state, queries, query_pos, keys, values, key_pos, scale):
    leading, total, summed = state
    scores = jnp.einsum("qhd,khd->qhk", queries, keys, preferred_element_type=jnp.float32) * scale
    visible = key_pos[None, None, :] <= query_pos[:, None, None]
    scores = jnp.where(visible, scores, NEGATIVE)
    new_leading = jnp.maximum(leading, jnp.max(scores, axis=2))
    shrink = jnp.exp(leading - new_leading)
    weights = jnp.where(visible, jnp.exp(scores - new_leading[:, :, None]), 0.0)
    total = total * shrink + jnp.sum(weights, axis=2)
    moved = jnp.einsum(
        "qhk,khd->qhd", weights.astype(jnp.bfloat16), values, preferred_element_type=jnp.float32
    )
    return (new_leading, total, summed * shrink[:, :, None] + moved)


def dense_heads(queries, keys, values, position_map):
    tok_rows, heads, width = queries.shape
    count = lax.axis_size("seq")
    half_rows = tok_rows // 2
    own_rows = lax.axis_index("seq") * tok_rows + jnp.arange(tok_rows, dtype=jnp.int32)
    query_pos = position_map(own_rows, tok_rows, count).reshape(2, half_rows)
    groups = queries.reshape(2, half_rows, heads, width)
    scale = 1.0 / math.sqrt(width)
    blank = (
        jnp.full((half_rows, heads), NEGATIVE, jnp.float32),
        jnp.zeros((half_rows, heads), jnp.float32),
        jnp.zeros((half_rows, heads, width), jnp.float32),
    )
    key_rows = lax.all_gather(keys, "seq", axis=0, tiled=True)
    value_rows = lax.all_gather(values, "seq", axis=0, tiled=True)
    length = key_rows.shape[0]
    block = math.gcd(length, 512)
    count_blocks = length // block
    key_pos = position_map(jnp.arange(length, dtype=jnp.int32), tok_rows, count).reshape(
        count_blocks, block
    )
    key_blocks = key_rows.reshape(count_blocks, block, heads, width)
    value_blocks = value_rows.reshape(count_blocks, block, heads, width)

    def advance(state, item):
        key_block, value_block, block_pos = item
        result = []
        for group in range(2):
            seen = jnp.min(block_pos) <= jnp.max(query_pos[group])
            result.append(
                lax.cond(
                    seen,
                    lambda inner, member=group: online_update(
                        inner,
                        groups[member],
                        query_pos[member],
                        key_block,
                        value_block,
                        block_pos,
                        scale,
                    ),
                    lambda inner: inner,
                    state[group],
                )
            )
        return (tuple(result), None)

    final_state, unused = lax.scan(advance, (blank, blank), (key_blocks, value_blocks, key_pos))
    outputs = [
        (summed / total[:, :, None]).astype(jnp.bfloat16) for leading, total, summed in final_state
    ]
    return jnp.concatenate(outputs, axis=0)


def attend_ranked(query_rows, query_ranks, keys, values, gate_rows):
    heads, rows, width = query_rows.shape
    block = math.gcd(rows, 512)
    scale = 1.0 / math.sqrt(width)
    key_ranks = jnp.arange(keys.shape[1], dtype=jnp.int32)

    def one_block(index):
        scores = (
            jnp.einsum("erd,ekd->erk", query_rows, keys, preferred_element_type=jnp.float32) * scale
        )
        visible = key_ranks[None, None, :] <= query_ranks[:, :, None]
        scores = jnp.where(visible, scores, NEGATIVE)
        leading = jnp.max(scores, axis=2, keepdims=True)
        weights = jnp.where(visible, jnp.exp(scores - leading), 0.0)
        total = jnp.sum(weights, axis=2, keepdims=True)
        mixed = (
            jnp.einsum(
                "erk,ekd->erd",
                weights.astype(jnp.bfloat16),
                values,
                preferred_element_type=jnp.float32,
            )
            / total
        )
        return (mixed * jax.nn.sigmoid(gate_rows.astype(jnp.float32))[:, :, None]).astype(
            jnp.bfloat16
        )

    blocks = lax.map(one_block, jnp.arange(rows // block, dtype=jnp.int32))
    return jnp.moveaxis(blocks, 0, 1).reshape(heads, rows, width)


def sparse_heads(queries, keys, values, gate_logit, selection):
    tok_rows, heads, width = queries.shape
    chosen = selection.shape[1]
    start = lax.axis_index("seq") * tok_rows
    positions = start + jnp.arange(tok_rows, dtype=jnp.int32)
    matches = selection[:, :, None] == positions[None, None, :]
    one_hot = matches.astype(jnp.bfloat16)

    def pick(source):
        return jnp.einsum(
            "ent,ted->end", one_hot, source, preferred_element_type=jnp.float32
        ).astype(jnp.bfloat16)

    gate_rows = jnp.einsum("ent,et->en", one_hot, gate_logit, preferred_element_type=jnp.float32)
    gathered = (
        lax.psum(pick(queries), "seq").astype(jnp.float32),
        lax.psum(pick(keys), "seq").astype(jnp.float32),
        lax.psum(pick(values), "seq").astype(jnp.float32),
        lax.psum(gate_rows.astype(jnp.bfloat16), "seq").astype(jnp.float32),
    )
    picked_q, picked_k, picked_v, picked_gate = [member.astype(jnp.bfloat16) for member in gathered]
    all_ranks = jnp.broadcast_to(jnp.arange(chosen, dtype=jnp.int32)[None, :], (heads, chosen))
    results = attend_ranked(picked_q, all_ranks, picked_k, picked_v, picked_gate)
    return jnp.einsum("ent,end->ted", one_hot, results, preferred_element_type=jnp.float32).astype(
        jnp.bfloat16
    )


def local(q_dense, k_dense, v_dense, q_expert, k_expert, v_expert, gate_logit, selection):
    dense_out = dense_heads(q_dense, k_dense, v_dense, plain_rows)
    expert_out = sparse_heads(q_expert, k_expert, v_expert, gate_logit, selection)
    return (dense_out, expert_out)

def nearest_pair(tok_rows, heads, width, experts, chosen):
    scale = math.log2(math.e) / math.sqrt(width)
    block = tok_rows // 2
    picks = experts * chosen
    contract_last = (((1,), (1,)), ((), ()))
    f32, bf16 = jnp.float32, jnp.bfloat16

    def kernel(
        q_ref, k_ref, v_ref, qe_ref, ke_ref, ve_ref, gate_hbm, sel_hbm,
        dense_ref, expert_ref,
        q_in, k_in, v_in, qe_in, ke_in, ve_in,
        wide, q_all, k_all, v_all, kf_all, vf_all, state, leading,
        picked, picked_far, gate_ref, sel_ref, in_sem, send_sem, recv_sem,
    ):
        me = lax.axis_index("seq")
        first = me == 0
        barrier = pltpu.get_barrier_semaphore()
        partner = {"seq": 1 - me}

        def far_copy(number, source, target):
            return pltpu.make_async_remote_copy(
                src_ref=source,
                dst_ref=target,
                send_sem=send_sem.at[number],
                recv_sem=recv_sem.at[number],
                device_id=partner,
                device_id_type=pl.DeviceIdType.MESH,
            )

        sent_k = far_copy(0, k_all, kf_all)
        sent_v = far_copy(1, v_all, vf_all)
        sent_picked = far_copy(2, picked, picked_far)

        @pl.when(me == 1)
        def _():
            pl.semaphore_signal(
                barrier, inc=1, device_id=partner, device_id_type=pl.DeviceIdType.MESH
            )

        loads = [
            pltpu.make_async_copy(source, target, in_sem.at[number])
            for number, (source, target) in enumerate(
                (
                    (k_ref, k_in),
                    (v_ref, v_in),
                    (sel_hbm, sel_ref),
                    (ke_ref, ke_in),
                    (ve_ref, ve_in),
                    (q_ref, q_in),
                    (qe_ref, qe_in),
                    (gate_hbm, gate_ref),
                )
            )
        ]
        for load in loads:
            load.start()

        def split(source, number, target):
            wide[number] = source[...].astype(f32)
            for head in range(heads):
                target[head] = wide[
                    number, pl.ds(head, tok_rows, stride=heads), :
                ].astype(bf16)

        def with_ones(values):
            return jnp.concatenate([values, jnp.ones_like(values)], axis=1)

        start = (me * tok_rows).astype(f32)

        def ready(*numbers):
            for number in numbers:
                loads[number].wait()

        def choose():
            chosen_rows = sel_ref[...].astype(f32)
            places = start + lax.broadcasted_iota(jnp.int32, (chosen, tok_rows), 1).astype(f32)
            one_hot = []
            for head in range(experts):
                square = jnp.broadcast_to(chosen_rows[head : head + 1, :], (chosen, chosen)).T
                one_hot.append(jnp.where(square[:, 0:1] == places, 1.0, 0.0).astype(bf16))
            return chosen_rows, one_hot

        def pick_pairs(one_hot):
            for head in range(experts):
                both = jnp.concatenate([ke_in[head], ve_in[head]], axis=1)
                picked[head * chosen : (head + 1) * chosen, :] = jnp.dot(
                    one_hot[head], both, preferred_element_type=f32
                ).astype(bf16)

        def local_scores(head, part):
            rows = slice(part * block, (part + 1) * block)
            scores = lax.dot_general(
                q_all[head, rows, :],
                k_all[head, 0 : (part + 1) * block, :],
                contract_last,
                preferred_element_type=f32,
            )
            edge = scores[:, part * block :]
            lower = lax.broadcasted_iota(jnp.int32, (block, block), 1) <= (
                lax.broadcasted_iota(jnp.int32, (block, block), 0)
            )
            edge = jnp.where(lower, edge, NEGATIVE)
            return edge if part == 0 else jnp.concatenate([scores[:, : part * block], edge], axis=1)

        def local_mix(head, part, scores):
            top = jnp.max(scores, axis=1, keepdims=True)
            weights = jnp.exp2((scores - top) * scale).astype(bf16)
            return top, jnp.dot(
                weights,
                with_ones(v_all[head, 0 : (part + 1) * block, :]),
                preferred_element_type=f32,
            )

        def far_scores(head, part):
            return lax.dot_general(
                q_all[head, part * block : (part + 1) * block, :],
                kf_all[head],
                contract_last,
                preferred_element_type=f32,
            )

        def far_mix(head, part, scores):
            rows = slice(part * block, (part + 1) * block)
            old = leading[head, rows, :]
            top = jnp.maximum(old, jnp.max(scores, axis=1, keepdims=True))
            weights = jnp.concatenate(
                [
                    jnp.exp2((scores[:, left : left + width] - top) * scale)
                    for left in range(0, tok_rows, width)
                ],
                axis=1,
            ).astype(bf16)
            shrink = jnp.exp2((old - top) * scale)
            return state[head, rows, :] * jnp.concatenate([shrink, shrink], axis=1) + jnp.dot(
                weights, with_ones(vf_all[head]), preferred_element_type=f32
            )

        def finish(head, part, mixed):
            wide[1, pl.ds(part * block * heads + head, block, stride=heads), :] = (
                mixed[:, 0:width] / mixed[:, width:]
            )

        def keep(head, part, top, mixed):
            rows = slice(part * block, (part + 1) * block)
            state[head, rows, :] = mixed
            leading[head, rows, :] = jnp.broadcast_to(top, (block, width))

        pieces = [(head, part) for head in range(heads) for part in range(2)]

        def staged(score, use):
            ready = [score(*pieces[0]), score(*pieces[1])]
            for number, piece in enumerate(pieces):
                if number + 2 < len(pieces):
                    ready.append(score(*pieces[number + 2]))
                use(*piece, ready[number])

        def expert_query(one_hot):
            query = jnp.concatenate(
                [
                    jnp.dot(one_hot[head], qe_in[head], preferred_element_type=f32)
                    for head in range(experts)
                ],
                axis=0,
            ).astype(bf16)
            logit = jnp.concatenate(
                [
                    jnp.sum(
                        one_hot[head].astype(f32) * gate_ref[head : head + 1, :].astype(f32),
                        axis=1,
                        keepdims=True,
                    )
                    for head in range(experts)
                ],
                axis=0,
            )
            return query, 1.0 + jnp.exp(-logit)

        def expert_result(query, gate, pairs):
            scores = lax.dot_general(
                query, pairs[:, 0:width], contract_last, preferred_element_type=f32
            )
            row_rank = lax.broadcasted_iota(jnp.int32, (picks, picks), 0)
            col_rank = lax.broadcasted_iota(jnp.int32, (picks, picks), 1)
            visible = jnp.logical_and(
                col_rank <= row_rank, col_rank // chosen == row_rank // chosen
            )
            scores = jnp.where(visible, scores, NEGATIVE)
            top = jnp.max(scores, axis=1, keepdims=True)
            weights = jnp.where(visible, jnp.exp2((scores - top) * scale), 0.0)
            total = jnp.sum(weights, axis=1, keepdims=True)
            mixed = jnp.dot(
                weights.astype(bf16), pairs[:, width:], preferred_element_type=f32
            )
            return (mixed / (total * gate)).astype(bf16)

        def expert_write(chosen_rows, result):
            token = start + lax.broadcasted_iota(jnp.int32, (tok_rows, chosen), 0).astype(f32)
            for head in range(experts):
                spread = jnp.where(
                    chosen_rows[head : head + 1, :] == token, 1.0, 0.0
                ).astype(bf16)
                expert_ref[head] = jnp.dot(
                    spread,
                    result[head * chosen : (head + 1) * chosen],
                    preferred_element_type=f32,
                ).astype(bf16)

        @pl.when(first)
        def _():
            ready(0)
            split(k_in, 0, k_all)
            pl.semaphore_wait(barrier, 1)
            sent_k.start()
            ready(1)
            split(v_in, 2, v_all)
            sent_v.start()
            ready(2, 3, 4)
            chosen_rows, one_hot = choose()
            pick_pairs(one_hot)
            sent_picked.start()
            ready(5, 6, 7)
            split(q_in, 1, q_all)
            result = expert_result(*expert_query(one_hot), picked[...])
            staged(
                local_scores,
                lambda head, part, scores: finish(head, part, local_mix(head, part, scores)[1]),
            )
            expert_write(chosen_rows, result)
            dense_ref[...] = wide[1].astype(bf16)

        @pl.when(me == 1)
        def _():
            ready(*range(8))
            split(k_in, 0, k_all)
            split(q_in, 1, q_all)
            chosen_rows, one_hot = choose()
            pick_pairs(one_hot)
            query, gate = expert_query(one_hot)
            split(v_in, 2, v_all)
            staged(
                local_scores,
                lambda head, part, scores: keep(head, part, *local_mix(head, part, scores)),
            )
            sent_k.wait_recv()
            sent_v.wait_recv()
            sent_picked.wait_recv()
            result = expert_result(query, gate, picked[...] + picked_far[...])
            staged(
                far_scores,
                lambda head, part, scores: finish(head, part, far_mix(head, part, scores)),
            )
            expert_write(chosen_rows, result)
            dense_ref[...] = wide[1].astype(bf16)

        @pl.when(first)
        def _():
            sent_k.wait_send()
            sent_v.wait_send()
            sent_picked.wait_send()

    in_hbm = pl.BlockSpec(memory_space=pltpu.HBM)
    in_vmem = pl.BlockSpec(memory_space=pltpu.VMEM)
    flat = (tok_rows * heads, width)
    return pl.pallas_call(
        kernel,
        out_shape=(
            pltpu.VMEM(flat, bf16),
            pltpu.VMEM((experts, tok_rows, width), bf16),
        ),
        in_specs=[in_hbm] * 8,
        out_specs=(in_vmem, in_vmem),
        scratch_shapes=[pltpu.VMEM(flat, bf16)] * 3
        + [pltpu.VMEM((experts, tok_rows, width), bf16)] * 3
        + [
            pltpu.VMEM((3,) + flat, f32),
            pltpu.VMEM((heads, tok_rows, width), bf16),
            pltpu.VMEM((heads, tok_rows, width), bf16),
            pltpu.VMEM((heads, tok_rows, width), bf16),
            pltpu.VMEM((heads, tok_rows, width), bf16),
            pltpu.VMEM((heads, tok_rows, width), bf16),
            pltpu.VMEM((heads, tok_rows, 2 * width), f32),
            pltpu.VMEM((heads, tok_rows, width), f32),
            pltpu.VMEM((picks, 2 * width), bf16),
            pltpu.VMEM((picks, 2 * width), bf16),
            pltpu.VMEM((experts, tok_rows), bf16),
            pltpu.VMEM((experts, chosen), jnp.int32),
            pltpu.SemaphoreType.DMA((8,)),
            pltpu.SemaphoreType.DMA((3,)),
            pltpu.SemaphoreType.DMA((3,)),
        ],
        compiler_params=pltpu.CompilerParams(
            collective_id=0, has_side_effects=True, vmem_limit_bytes=32 * 1024 * 1024
        ),
    )


def write_out(dense, expert):
    def kernel(dense_ref, expert_ref, dense_out, expert_out, sems):
        copies = [
            pltpu.make_async_copy(expert_ref, expert_out, sems.at[0]),
            pltpu.make_async_copy(dense_ref, dense_out, sems.at[1]),
        ]
        for copy in copies:
            copy.start()
        for copy in copies:
            copy.wait()

    return pl.pallas_call(
        kernel,
        out_shape=tuple(
            pltpu.HBM(member.shape, member.dtype) for member in (dense, expert)
        ),
        in_specs=[pl.BlockSpec(memory_space=pltpu.VMEM)] * 2,
        out_specs=tuple([pl.BlockSpec(memory_space=pltpu.HBM)] * 2),
        scratch_shapes=[pltpu.SemaphoreType.DMA((2,))],
        compiler_params=pltpu.CompilerParams(vmem_limit_bytes=4 * 1024 * 1024),
    )(
        pltpu.with_memory_space_constraint(dense, pltpu.VMEM),
        pltpu.with_memory_space_constraint(expert, pltpu.VMEM),
    )


def local_pair(q_dense, k_dense, v_dense, q_expert, k_expert, v_expert, gate_logit, selection):
    tok_rows, heads, width = q_dense.shape
    experts, chosen = selection.shape
    call = nearest_pair(tok_rows, heads, width, experts, chosen)
    dense_out, expert_out = call(
        *(
            pltpu.with_memory_space_constraint(member, pltpu.HBM)
            for member in (
                q_dense.reshape(tok_rows * heads, width),
                k_dense.reshape(tok_rows * heads, width),
                v_dense.reshape(tok_rows * heads, width),
                jnp.transpose(q_expert, (1, 0, 2)),
                jnp.transpose(k_expert, (1, 0, 2)),
                jnp.transpose(v_expert, (1, 0, 2)),
                gate_logit,
                selection,
            )
        )
    )
    dense_out, expert_out = write_out(dense_out, expert_out)
    return (dense_out.reshape(tok_rows, heads, width), jnp.transpose(expert_out, (1, 0, 2)))


def solution(mesh):
    placed = (
        P(("dp", "seq"), "head", None),
        P(("dp", "seq"), "head", None),
        P(("dp", "seq"), "head", None),
        P(("dp", "seq"), "head", None),
        P(("dp", "seq"), "head", None),
        P(("dp", "seq"), "head", None),
        P("head", ("dp", "seq")),
        P("head", "dp"),
    )
    return jax.shard_map(
        local_pair if mesh.shape["seq"] == 2 else local,
        mesh=mesh,
        in_specs=placed,
        out_specs=(P(("dp", "seq"), "head", None), P(("dp", "seq"), "head", None)),
        check_vma=False,
    )
```

```python
import math

import jax
import jax.numpy as jnp
from jax import lax
from jax.experimental import pallas as pl
from jax.experimental.pallas import tpu as pltpu
from jax.sharding import PartitionSpec as P

NEGATIVE = -1e30


def plain_rows(rows, tok_rows, count):
    return rows


def online_update(state, queries, query_pos, keys, values, key_pos, scale):
    leading, total, summed = state
    scores = jnp.einsum("qhd,khd->qhk", queries, keys, preferred_element_type=jnp.float32) * scale
    visible = key_pos[None, None, :] <= query_pos[:, None, None]
    scores = jnp.where(visible, scores, NEGATIVE)
    new_leading = jnp.maximum(leading, jnp.max(scores, axis=2))
    shrink = jnp.exp(leading - new_leading)
    weights = jnp.where(visible, jnp.exp(scores - new_leading[:, :, None]), 0.0)
    total = total * shrink + jnp.sum(weights, axis=2)
    moved = jnp.einsum(
        "qhk,khd->qhd", weights.astype(jnp.bfloat16), values, preferred_element_type=jnp.float32
    )
    return (new_leading, total, summed * shrink[:, :, None] + moved)


def dense_heads(queries, keys, values, position_map):
    tok_rows, heads, width = queries.shape
    count = lax.axis_size("seq")
    half_rows = tok_rows // 2
    own_rows = lax.axis_index("seq") * tok_rows + jnp.arange(tok_rows, dtype=jnp.int32)
    query_pos = position_map(own_rows, tok_rows, count).reshape(2, half_rows)
    groups = queries.reshape(2, half_rows, heads, width)
    scale = 1.0 / math.sqrt(width)
    blank = (
        jnp.full((half_rows, heads), NEGATIVE, jnp.float32),
        jnp.zeros((half_rows, heads), jnp.float32),
        jnp.zeros((half_rows, heads, width), jnp.float32),
    )
    key_rows = lax.all_gather(keys, "seq", axis=0, tiled=True)
    value_rows = lax.all_gather(values, "seq", axis=0, tiled=True)
    length = key_rows.shape[0]
    block = math.gcd(length, 512)
    count_blocks = length // block
    key_pos = position_map(jnp.arange(length, dtype=jnp.int32), tok_rows, count).reshape(
        count_blocks, block
    )
    key_blocks = key_rows.reshape(count_blocks, block, heads, width)
    value_blocks = value_rows.reshape(count_blocks, block, heads, width)

    def advance(state, item):
        key_block, value_block, block_pos = item
        result = []
        for group in range(2):
            seen = jnp.min(block_pos) <= jnp.max(query_pos[group])
            result.append(
                lax.cond(
                    seen,
                    lambda inner, member=group: online_update(
                        inner,
                        groups[member],
                        query_pos[member],
                        key_block,
                        value_block,
                        block_pos,
                        scale,
                    ),
                    lambda inner: inner,
                    state[group],
                )
            )
        return (tuple(result), None)

    final_state, unused = lax.scan(advance, (blank, blank), (key_blocks, value_blocks, key_pos))
    outputs = [
        (summed / total[:, :, None]).astype(jnp.bfloat16) for leading, total, summed in final_state
    ]
    return jnp.concatenate(outputs, axis=0)


def attend_ranked(query_rows, query_ranks, keys, values, gate_rows):
    heads, rows, width = query_rows.shape
    block = math.gcd(rows, 512)
    scale = 1.0 / math.sqrt(width)
    key_ranks = jnp.arange(keys.shape[1], dtype=jnp.int32)

    def one_block(index):
        scores = (
            jnp.einsum("erd,ekd->erk", query_rows, keys, preferred_element_type=jnp.float32) * scale
        )
        visible = key_ranks[None, None, :] <= query_ranks[:, :, None]
        scores = jnp.where(visible, scores, NEGATIVE)
        leading = jnp.max(scores, axis=2, keepdims=True)
        weights = jnp.where(visible, jnp.exp(scores - leading), 0.0)
        total = jnp.sum(weights, axis=2, keepdims=True)
        mixed = (
            jnp.einsum(
                "erk,ekd->erd",
                weights.astype(jnp.bfloat16),
                values,
                preferred_element_type=jnp.float32,
            )
            / total
        )
        return (mixed * jax.nn.sigmoid(gate_rows.astype(jnp.float32))[:, :, None]).astype(
            jnp.bfloat16
        )

    blocks = lax.map(one_block, jnp.arange(rows // block, dtype=jnp.int32))
    return jnp.moveaxis(blocks, 0, 1).reshape(heads, rows, width)


def sparse_heads(queries, keys, values, gate_logit, selection):
    tok_rows, heads, width = queries.shape
    chosen = selection.shape[1]
    start = lax.axis_index("seq") * tok_rows
    positions = start + jnp.arange(tok_rows, dtype=jnp.int32)
    matches = selection[:, :, None] == positions[None, None, :]
    one_hot = matches.astype(jnp.bfloat16)

    def pick(source):
        return jnp.einsum(
            "ent,ted->end", one_hot, source, preferred_element_type=jnp.float32
        ).astype(jnp.bfloat16)

    gate_rows = jnp.einsum("ent,et->en", one_hot, gate_logit, preferred_element_type=jnp.float32)
    gathered = (
        lax.psum(pick(queries), "seq").astype(jnp.float32),
        lax.psum(pick(keys), "seq").astype(jnp.float32),
        lax.psum(pick(values), "seq").astype(jnp.float32),
        lax.psum(gate_rows.astype(jnp.bfloat16), "seq").astype(jnp.float32),
    )
    picked_q, picked_k, picked_v, picked_gate = [member.astype(jnp.bfloat16) for member in gathered]
    all_ranks = jnp.broadcast_to(jnp.arange(chosen, dtype=jnp.int32)[None, :], (heads, chosen))
    results = attend_ranked(picked_q, all_ranks, picked_k, picked_v, picked_gate)
    return jnp.einsum("ent,end->ted", one_hot, results, preferred_element_type=jnp.float32).astype(
        jnp.bfloat16
    )


def local(q_dense, k_dense, v_dense, q_expert, k_expert, v_expert, gate_logit, selection):
    dense_out = dense_heads(q_dense, k_dense, v_dense, plain_rows)
    expert_out = sparse_heads(q_expert, k_expert, v_expert, gate_logit, selection)
    return (dense_out, expert_out)

def nearest_pair(tok_rows, heads, width, experts, chosen):
    scale = math.log2(math.e) / math.sqrt(width)
    block = tok_rows // 2
    picks = experts * chosen
    contract_last = (((1,), (1,)), ((), ()))
    f32, bf16 = jnp.float32, jnp.bfloat16

    def kernel(
        q_ref, k_ref, v_ref, qe_ref, ke_ref, ve_ref, gate_hbm, sel_hbm,
        dense_ref, expert_ref,
        q_in, k_in, v_in, qe_in, ke_in, ve_in,
        wide, q_all, k_all, v_all, kf_all, vf_all, state, leading,
        picked, picked_far, gate_ref, sel_ref, in_sem, send_sem, recv_sem,
    ):
        me = lax.axis_index("seq")
        first = me == 0
        barrier = pltpu.get_barrier_semaphore()
        partner = {"seq": 1 - me}

        def far_copy(number, source, target):
            return pltpu.make_async_remote_copy(
                src_ref=source,
                dst_ref=target,
                send_sem=send_sem.at[number],
                recv_sem=recv_sem.at[number],
                device_id=partner,
                device_id_type=pl.DeviceIdType.MESH,
            )

        sent_k = far_copy(0, k_all, kf_all)
        sent_v = far_copy(1, v_all, vf_all)
        sent_picked = far_copy(2, picked, picked_far)

        @pl.when(me == 1)
        def _():
            pl.semaphore_signal(
                barrier, inc=1, device_id=partner, device_id_type=pl.DeviceIdType.MESH
            )

        loads = [
            pltpu.make_async_copy(source, target, in_sem.at[number])
            for number, (source, target) in enumerate(
                (
                    (k_ref, k_in),
                    (v_ref, v_in),
                    (q_ref, q_in),
                    (sel_hbm, sel_ref),
                    (ke_ref, ke_in),
                    (ve_ref, ve_in),
                    (qe_ref, qe_in),
                    (gate_hbm, gate_ref),
                )
            )
        ]
        for load in loads:
            load.start()

        def split(source, number, target):
            wide[number] = source[...].astype(f32)
            for head in range(heads):
                target[head] = wide[
                    number, pl.ds(head, tok_rows, stride=heads), :
                ].astype(bf16)

        def with_ones(values):
            return jnp.concatenate([values, jnp.ones_like(values)], axis=1)

        start = (me * tok_rows).astype(f32)

        def ready(*numbers):
            for number in numbers:
                loads[number].wait()

        def choose():
            chosen_rows = sel_ref[...].astype(f32)
            places = start + lax.broadcasted_iota(jnp.int32, (chosen, tok_rows), 1).astype(f32)
            one_hot = []
            for head in range(experts):
                square = jnp.broadcast_to(chosen_rows[head : head + 1, :], (chosen, chosen)).T
                one_hot.append(jnp.where(square[:, 0:1] == places, 1.0, 0.0).astype(bf16))
            return chosen_rows, one_hot

        def pick_pairs(one_hot):
            for head in range(experts):
                both = jnp.concatenate([ke_in[head], ve_in[head]], axis=1)
                picked[head * chosen : (head + 1) * chosen, :] = jnp.dot(
                    one_hot[head], both, preferred_element_type=f32
                ).astype(bf16)

        def local_scores(head, part):
            rows = slice(part * block, (part + 1) * block)
            scores = lax.dot_general(
                q_all[head, rows, :],
                k_all[head, 0 : (part + 1) * block, :],
                contract_last,
                preferred_element_type=f32,
            )
            edge = scores[:, part * block :]
            lower = lax.broadcasted_iota(jnp.int32, (block, block), 1) <= (
                lax.broadcasted_iota(jnp.int32, (block, block), 0)
            )
            edge = jnp.where(lower, edge, NEGATIVE)
            return edge if part == 0 else jnp.concatenate([scores[:, : part * block], edge], axis=1)

        def local_mix(head, part, scores):
            top = jnp.max(scores, axis=1, keepdims=True)
            weights = jnp.exp2((scores - top) * scale).astype(bf16)
            return top, jnp.dot(
                weights,
                with_ones(v_all[head, 0 : (part + 1) * block, :]),
                preferred_element_type=f32,
            )

        def far_scores(head, part):
            return lax.dot_general(
                q_all[head, part * block : (part + 1) * block, :],
                kf_all[head],
                contract_last,
                preferred_element_type=f32,
            )

        def far_mix(head, part, scores):
            rows = slice(part * block, (part + 1) * block)
            old = leading[head, rows, :]
            top = jnp.maximum(old, jnp.max(scores, axis=1, keepdims=True))
            weights = jnp.concatenate(
                [
                    jnp.exp2((scores[:, left : left + width] - top) * scale)
                    for left in range(0, tok_rows, width)
                ],
                axis=1,
            ).astype(bf16)
            shrink = jnp.exp2((old - top) * scale)
            return state[head, rows, :] * jnp.concatenate([shrink, shrink], axis=1) + jnp.dot(
                weights, with_ones(vf_all[head]), preferred_element_type=f32
            )

        def finish(head, part, mixed):
            wide[1, pl.ds(part * block * heads + head, block, stride=heads), :] = (
                mixed[:, 0:width] / mixed[:, width:]
            )

        def keep(head, part, top, mixed):
            rows = slice(part * block, (part + 1) * block)
            state[head, rows, :] = mixed
            leading[head, rows, :] = jnp.broadcast_to(top, (block, width))

        pieces = [(head, part) for head in range(heads) for part in range(2)]

        def staged(score, use):
            ready = [score(*pieces[0]), score(*pieces[1])]
            for number, piece in enumerate(pieces):
                if number + 2 < len(pieces):
                    ready.append(score(*pieces[number + 2]))
                use(*piece, ready[number])

        def expert_query(one_hot):
            query = jnp.concatenate(
                [
                    jnp.dot(one_hot[head], qe_in[head], preferred_element_type=f32)
                    for head in range(experts)
                ],
                axis=0,
            ).astype(bf16)
            logit = jnp.concatenate(
                [
                    jnp.sum(
                        one_hot[head].astype(f32) * gate_ref[head : head + 1, :].astype(f32),
                        axis=1,
                        keepdims=True,
                    )
                    for head in range(experts)
                ],
                axis=0,
            )
            return query, 1.0 + jnp.exp(-logit)

        def expert_result(query, gate, pairs):
            scores = lax.dot_general(
                query, pairs[:, 0:width], contract_last, preferred_element_type=f32
            )
            row_rank = lax.broadcasted_iota(jnp.int32, (picks, picks), 0)
            col_rank = lax.broadcasted_iota(jnp.int32, (picks, picks), 1)
            visible = jnp.logical_and(
                col_rank <= row_rank, col_rank // chosen == row_rank // chosen
            )
            scores = jnp.where(visible, scores, NEGATIVE)
            top = jnp.max(scores, axis=1, keepdims=True)
            weights = jnp.where(visible, jnp.exp2((scores - top) * scale), 0.0)
            total = jnp.sum(weights, axis=1, keepdims=True)
            mixed = jnp.dot(
                weights.astype(bf16), pairs[:, width:], preferred_element_type=f32
            )
            return (mixed / (total * gate)).astype(bf16)

        def spreads(chosen_rows):
            token = start + lax.broadcasted_iota(jnp.int32, (tok_rows, chosen), 0).astype(f32)
            return [
                jnp.where(chosen_rows[head : head + 1, :] == token, 1.0, 0.0).astype(bf16)
                for head in range(experts)
            ]

        def expert_write(spread, result):
            for head in range(experts):
                expert_ref[head] = jnp.dot(
                    spread[head],
                    result[head * chosen : (head + 1) * chosen],
                    preferred_element_type=f32,
                ).astype(bf16)

        @pl.when(first)
        def _():
            ready(0)
            split(k_in, 0, k_all)
            pl.semaphore_wait(barrier, 1)
            sent_k.start()
            ready(1)
            split(v_in, 2, v_all)
            sent_v.start()
            ready(3, 4, 5)
            chosen_rows, one_hot = choose()
            pick_pairs(one_hot)
            sent_picked.start()
            ready(2, 6, 7)
            split(q_in, 1, q_all)
            result = expert_result(*expert_query(one_hot), picked[...])
            staged(
                local_scores,
                lambda head, part, scores: finish(head, part, local_mix(head, part, scores)[1]),
            )
            expert_write(spreads(chosen_rows), result)
            dense_ref[...] = wide[1].astype(bf16)

        @pl.when(me == 1)
        def _():
            ready(0, 1, 2)
            split(k_in, 0, k_all)
            split(q_in, 1, q_all)
            split(v_in, 2, v_all)
            staged(
                local_scores,
                lambda head, part, scores: keep(head, part, *local_mix(head, part, scores)),
            )
            ready(3, 4, 5, 6, 7)
            chosen_rows, one_hot = choose()
            pick_pairs(one_hot)
            query, gate = expert_query(one_hot)
            spread = spreads(chosen_rows)
            sent_k.wait_recv()
            sent_v.wait_recv()
            sent_picked.wait_recv()
            result = expert_result(query, gate, picked[...] + picked_far[...])
            staged(
                far_scores,
                lambda head, part, scores: finish(head, part, far_mix(head, part, scores)),
            )
            expert_write(spread, result)
            dense_ref[...] = wide[1].astype(bf16)

        @pl.when(first)
        def _():
            sent_k.wait_send()
            sent_v.wait_send()
            sent_picked.wait_send()

    in_hbm = pl.BlockSpec(memory_space=pltpu.HBM)
    in_vmem = pl.BlockSpec(memory_space=pltpu.VMEM)
    flat = (tok_rows * heads, width)
    return pl.pallas_call(
        kernel,
        out_shape=(
            pltpu.VMEM(flat, bf16),
            pltpu.VMEM((experts, tok_rows, width), bf16),
        ),
        in_specs=[in_hbm] * 8,
        out_specs=(in_vmem, in_vmem),
        scratch_shapes=[pltpu.VMEM(flat, bf16)] * 3
        + [pltpu.VMEM((experts, tok_rows, width), bf16)] * 3
        + [
            pltpu.VMEM((3,) + flat, f32),
            pltpu.VMEM((heads, tok_rows, width), bf16),
            pltpu.VMEM((heads, tok_rows, width), bf16),
            pltpu.VMEM((heads, tok_rows, width), bf16),
            pltpu.VMEM((heads, tok_rows, width), bf16),
            pltpu.VMEM((heads, tok_rows, width), bf16),
            pltpu.VMEM((heads, tok_rows, 2 * width), f32),
            pltpu.VMEM((heads, tok_rows, width), f32),
            pltpu.VMEM((picks, 2 * width), bf16),
            pltpu.VMEM((picks, 2 * width), bf16),
            pltpu.VMEM((experts, tok_rows), bf16),
            pltpu.VMEM((experts, chosen), jnp.int32),
            pltpu.SemaphoreType.DMA((8,)),
            pltpu.SemaphoreType.DMA((3,)),
            pltpu.SemaphoreType.DMA((3,)),
        ],
        compiler_params=pltpu.CompilerParams(
            collective_id=0, has_side_effects=True, vmem_limit_bytes=32 * 1024 * 1024
        ),
    )


def write_out(dense, expert):
    def kernel(dense_ref, expert_ref, dense_out, expert_out, sems):
        copies = [
            pltpu.make_async_copy(expert_ref, expert_out, sems.at[0]),
            pltpu.make_async_copy(dense_ref, dense_out, sems.at[1]),
        ]
        for copy in copies:
            copy.start()
        for copy in copies:
            copy.wait()

    return pl.pallas_call(
        kernel,
        out_shape=tuple(
            pltpu.HBM(member.shape, member.dtype) for member in (dense, expert)
        ),
        in_specs=[pl.BlockSpec(memory_space=pltpu.VMEM)] * 2,
        out_specs=tuple([pl.BlockSpec(memory_space=pltpu.HBM)] * 2),
        scratch_shapes=[pltpu.SemaphoreType.DMA((2,))],
        compiler_params=pltpu.CompilerParams(vmem_limit_bytes=4 * 1024 * 1024),
    )(
        pltpu.with_memory_space_constraint(dense, pltpu.VMEM),
        pltpu.with_memory_space_constraint(expert, pltpu.VMEM),
    )


def local_pair(q_dense, k_dense, v_dense, q_expert, k_expert, v_expert, gate_logit, selection):
    tok_rows, heads, width = q_dense.shape
    experts, chosen = selection.shape
    call = nearest_pair(tok_rows, heads, width, experts, chosen)
    dense_out, expert_out = call(
        *(
            pltpu.with_memory_space_constraint(member, pltpu.HBM)
            for member in (
                q_dense.reshape(tok_rows * heads, width),
                k_dense.reshape(tok_rows * heads, width),
                v_dense.reshape(tok_rows * heads, width),
                jnp.transpose(q_expert, (1, 0, 2)),
                jnp.transpose(k_expert, (1, 0, 2)),
                jnp.transpose(v_expert, (1, 0, 2)),
                gate_logit,
                selection,
            )
        )
    )
    dense_out, expert_out = write_out(dense_out, expert_out)
    return (dense_out.reshape(tok_rows, heads, width), jnp.transpose(expert_out, (1, 0, 2)))


def solution(mesh):
    placed = (
        P(("dp", "seq"), "head", None),
        P(("dp", "seq"), "head", None),
        P(("dp", "seq"), "head", None),
        P(("dp", "seq"), "head", None),
        P(("dp", "seq"), "head", None),
        P(("dp", "seq"), "head", None),
        P("head", ("dp", "seq")),
        P("head", "dp"),
    )
    return jax.shard_map(
        local_pair if mesh.shape["seq"] == 2 else local,
        mesh=mesh,
        in_specs=placed,
        out_specs=(P(("dp", "seq"), "head", None), P(("dp", "seq"), "head", None)),
        check_vma=False,
    )
```

```python
import math

import jax
import jax.numpy as jnp
from jax import lax
from jax.experimental import pallas as pl
from jax.experimental.pallas import tpu as pltpu
from jax.sharding import PartitionSpec as P

NEGATIVE = -1e30


def plain_rows(rows, tok_rows, count):
    return rows


def online_update(state, queries, query_pos, keys, values, key_pos, scale):
    leading, total, summed = state
    scores = jnp.einsum("qhd,khd->qhk", queries, keys, preferred_element_type=jnp.float32) * scale
    visible = key_pos[None, None, :] <= query_pos[:, None, None]
    scores = jnp.where(visible, scores, NEGATIVE)
    new_leading = jnp.maximum(leading, jnp.max(scores, axis=2))
    shrink = jnp.exp(leading - new_leading)
    weights = jnp.where(visible, jnp.exp(scores - new_leading[:, :, None]), 0.0)
    total = total * shrink + jnp.sum(weights, axis=2)
    moved = jnp.einsum(
        "qhk,khd->qhd", weights.astype(jnp.bfloat16), values, preferred_element_type=jnp.float32
    )
    return (new_leading, total, summed * shrink[:, :, None] + moved)


def dense_heads(queries, keys, values, position_map):
    tok_rows, heads, width = queries.shape
    count = lax.axis_size("seq")
    half_rows = tok_rows // 2
    own_rows = lax.axis_index("seq") * tok_rows + jnp.arange(tok_rows, dtype=jnp.int32)
    query_pos = position_map(own_rows, tok_rows, count).reshape(2, half_rows)
    groups = queries.reshape(2, half_rows, heads, width)
    scale = 1.0 / math.sqrt(width)
    blank = (
        jnp.full((half_rows, heads), NEGATIVE, jnp.float32),
        jnp.zeros((half_rows, heads), jnp.float32),
        jnp.zeros((half_rows, heads, width), jnp.float32),
    )
    key_rows = lax.all_gather(keys, "seq", axis=0, tiled=True)
    value_rows = lax.all_gather(values, "seq", axis=0, tiled=True)
    length = key_rows.shape[0]
    block = math.gcd(length, 512)
    count_blocks = length // block
    key_pos = position_map(jnp.arange(length, dtype=jnp.int32), tok_rows, count).reshape(
        count_blocks, block
    )
    key_blocks = key_rows.reshape(count_blocks, block, heads, width)
    value_blocks = value_rows.reshape(count_blocks, block, heads, width)

    def advance(state, item):
        key_block, value_block, block_pos = item
        result = []
        for group in range(2):
            seen = jnp.min(block_pos) <= jnp.max(query_pos[group])
            result.append(
                lax.cond(
                    seen,
                    lambda inner, member=group: online_update(
                        inner,
                        groups[member],
                        query_pos[member],
                        key_block,
                        value_block,
                        block_pos,
                        scale,
                    ),
                    lambda inner: inner,
                    state[group],
                )
            )
        return (tuple(result), None)

    final_state, unused = lax.scan(advance, (blank, blank), (key_blocks, value_blocks, key_pos))
    outputs = [
        (summed / total[:, :, None]).astype(jnp.bfloat16) for leading, total, summed in final_state
    ]
    return jnp.concatenate(outputs, axis=0)


def attend_ranked(query_rows, query_ranks, keys, values, gate_rows):
    heads, rows, width = query_rows.shape
    block = math.gcd(rows, 512)
    scale = 1.0 / math.sqrt(width)
    key_ranks = jnp.arange(keys.shape[1], dtype=jnp.int32)

    def one_block(index):
        scores = (
            jnp.einsum("erd,ekd->erk", query_rows, keys, preferred_element_type=jnp.float32) * scale
        )
        visible = key_ranks[None, None, :] <= query_ranks[:, :, None]
        scores = jnp.where(visible, scores, NEGATIVE)
        leading = jnp.max(scores, axis=2, keepdims=True)
        weights = jnp.where(visible, jnp.exp(scores - leading), 0.0)
        total = jnp.sum(weights, axis=2, keepdims=True)
        mixed = (
            jnp.einsum(
                "erk,ekd->erd",
                weights.astype(jnp.bfloat16),
                values,
                preferred_element_type=jnp.float32,
            )
            / total
        )
        return (mixed * jax.nn.sigmoid(gate_rows.astype(jnp.float32))[:, :, None]).astype(
            jnp.bfloat16
        )

    blocks = lax.map(one_block, jnp.arange(rows // block, dtype=jnp.int32))
    return jnp.moveaxis(blocks, 0, 1).reshape(heads, rows, width)


def sparse_heads(queries, keys, values, gate_logit, selection):
    tok_rows, heads, width = queries.shape
    chosen = selection.shape[1]
    start = lax.axis_index("seq") * tok_rows
    positions = start + jnp.arange(tok_rows, dtype=jnp.int32)
    matches = selection[:, :, None] == positions[None, None, :]
    one_hot = matches.astype(jnp.bfloat16)

    def pick(source):
        return jnp.einsum(
            "ent,ted->end", one_hot, source, preferred_element_type=jnp.float32
        ).astype(jnp.bfloat16)

    gate_rows = jnp.einsum("ent,et->en", one_hot, gate_logit, preferred_element_type=jnp.float32)
    gathered = (
        lax.psum(pick(queries), "seq").astype(jnp.float32),
        lax.psum(pick(keys), "seq").astype(jnp.float32),
        lax.psum(pick(values), "seq").astype(jnp.float32),
        lax.psum(gate_rows.astype(jnp.bfloat16), "seq").astype(jnp.float32),
    )
    picked_q, picked_k, picked_v, picked_gate = [member.astype(jnp.bfloat16) for member in gathered]
    all_ranks = jnp.broadcast_to(jnp.arange(chosen, dtype=jnp.int32)[None, :], (heads, chosen))
    results = attend_ranked(picked_q, all_ranks, picked_k, picked_v, picked_gate)
    return jnp.einsum("ent,end->ted", one_hot, results, preferred_element_type=jnp.float32).astype(
        jnp.bfloat16
    )


def local(q_dense, k_dense, v_dense, q_expert, k_expert, v_expert, gate_logit, selection):
    dense_out = dense_heads(q_dense, k_dense, v_dense, plain_rows)
    expert_out = sparse_heads(q_expert, k_expert, v_expert, gate_logit, selection)
    return (dense_out, expert_out)

def nearest_pair(tok_rows, heads, width, experts, chosen):
    scale = math.log2(math.e) / math.sqrt(width)
    block = tok_rows // 2
    picks = experts * chosen
    contract_last = (((1,), (1,)), ((), ()))
    f32, bf16 = jnp.float32, jnp.bfloat16

    def kernel(
        q_ref, k_ref, v_ref, qe_ref, ke_ref, ve_ref, gate_hbm, sel_hbm,
        dense_ref, expert_ref,
        q_in, k_in, v_in, k_far, v_far, qe_in, ke_in, ve_in,
        wide, q_all, k_all, v_all, kf_all, vf_all, state, leading,
        picked, picked_far, gate_ref, sel_ref, in_sem, send_sem, recv_sem,
    ):
        me = lax.axis_index("seq")
        first = me == 0
        barrier = pltpu.get_barrier_semaphore()
        partner = {"seq": 1 - me}

        def far_copy(number, source, target):
            return pltpu.make_async_remote_copy(
                src_ref=source,
                dst_ref=target,
                send_sem=send_sem.at[number],
                recv_sem=recv_sem.at[number],
                device_id=partner,
                device_id_type=pl.DeviceIdType.MESH,
            )

        sent_k = far_copy(0, k_ref, k_far)
        sent_v = far_copy(1, v_ref, v_far)
        sent_picked = far_copy(2, picked, picked_far)

        @pl.when(me == 1)
        def _():
            pl.semaphore_signal(
                barrier, inc=1, device_id=partner, device_id_type=pl.DeviceIdType.MESH
            )

        loads = [
            pltpu.make_async_copy(source, target, in_sem.at[number])
            for number, (source, target) in enumerate(
                (
                    (k_ref, k_in),
                    (v_ref, v_in),
                    (q_ref, q_in),
                    (sel_hbm, sel_ref),
                    (ke_ref, ke_in),
                    (ve_ref, ve_in),
                    (qe_ref, qe_in),
                    (gate_hbm, gate_ref),
                )
            )
        ]
        def begin(*numbers):
            for number in numbers:
                loads[number].start()

        def split(source, number, target):
            wide[number] = source[...].astype(f32)
            for head in range(heads):
                target[head] = wide[
                    number, pl.ds(head, tok_rows, stride=heads), :
                ].astype(bf16)

        def with_ones(values):
            return jnp.concatenate([values, jnp.ones_like(values)], axis=1)

        start = (me * tok_rows).astype(f32)

        def ready(*numbers):
            for number in numbers:
                loads[number].wait()

        def choose():
            chosen_rows = sel_ref[...].astype(f32)
            places = start + lax.broadcasted_iota(jnp.int32, (chosen, tok_rows), 1).astype(f32)
            one_hot = []
            for head in range(experts):
                square = jnp.broadcast_to(chosen_rows[head : head + 1, :], (chosen, chosen)).T
                one_hot.append(jnp.where(square[:, 0:1] == places, 1.0, 0.0).astype(bf16))
            return chosen_rows, one_hot

        def pick_pairs(one_hot):
            for head in range(experts):
                both = jnp.concatenate([ke_in[head], ve_in[head]], axis=1)
                picked[head * chosen : (head + 1) * chosen, :] = jnp.dot(
                    one_hot[head], both, preferred_element_type=f32
                ).astype(bf16)

        def local_scores(head, part):
            rows = slice(part * block, (part + 1) * block)
            scores = lax.dot_general(
                q_all[head, rows, :],
                k_all[head, 0 : (part + 1) * block, :],
                contract_last,
                preferred_element_type=f32,
            )
            edge = scores[:, part * block :]
            lower = lax.broadcasted_iota(jnp.int32, (block, block), 1) <= (
                lax.broadcasted_iota(jnp.int32, (block, block), 0)
            )
            edge = jnp.where(lower, edge, NEGATIVE)
            return edge if part == 0 else jnp.concatenate([scores[:, : part * block], edge], axis=1)

        def local_mix(head, part, scores):
            top = jnp.max(scores, axis=1, keepdims=True)
            weights = jnp.exp2((scores - top) * scale).astype(bf16)
            return top, jnp.dot(
                weights,
                with_ones(v_all[head, 0 : (part + 1) * block, :]),
                preferred_element_type=f32,
            )

        def far_scores(head, part):
            return lax.dot_general(
                q_all[head, part * block : (part + 1) * block, :],
                kf_all[head],
                contract_last,
                preferred_element_type=f32,
            )

        def far_mix(head, part, scores):
            rows = slice(part * block, (part + 1) * block)
            old = leading[head, rows, :]
            top = jnp.maximum(old, jnp.max(scores, axis=1, keepdims=True))
            weights = jnp.concatenate(
                [
                    jnp.exp2((scores[:, left : left + width] - top) * scale)
                    for left in range(0, tok_rows, width)
                ],
                axis=1,
            ).astype(bf16)
            shrink = jnp.exp2((old - top) * scale)
            return state[head, rows, :] * jnp.concatenate([shrink, shrink], axis=1) + jnp.dot(
                weights, with_ones(vf_all[head]), preferred_element_type=f32
            )

        def finish(head, part, mixed):
            wide[1, pl.ds(part * block * heads + head, block, stride=heads), :] = (
                mixed[:, 0:width] / mixed[:, width:]
            )

        def keep(head, part, top, mixed):
            rows = slice(part * block, (part + 1) * block)
            state[head, rows, :] = mixed
            leading[head, rows, :] = jnp.broadcast_to(top, (block, width))

        pieces = [(head, part) for head in range(heads) for part in range(2)]

        def staged(score, use):
            ready = [score(*pieces[0]), score(*pieces[1])]
            for number, piece in enumerate(pieces):
                if number + 2 < len(pieces):
                    ready.append(score(*pieces[number + 2]))
                use(*piece, ready[number])

        def expert_query(one_hot):
            query = jnp.concatenate(
                [
                    jnp.dot(one_hot[head], qe_in[head], preferred_element_type=f32)
                    for head in range(experts)
                ],
                axis=0,
            ).astype(bf16)
            logit = jnp.concatenate(
                [
                    jnp.sum(
                        one_hot[head].astype(f32) * gate_ref[head : head + 1, :].astype(f32),
                        axis=1,
                        keepdims=True,
                    )
                    for head in range(experts)
                ],
                axis=0,
            )
            return query, 1.0 + jnp.exp(-logit)

        def expert_result(query, gate, pairs):
            scores = lax.dot_general(
                query, pairs[:, 0:width], contract_last, preferred_element_type=f32
            )
            row_rank = lax.broadcasted_iota(jnp.int32, (picks, picks), 0)
            col_rank = lax.broadcasted_iota(jnp.int32, (picks, picks), 1)
            visible = jnp.logical_and(
                col_rank <= row_rank, col_rank // chosen == row_rank // chosen
            )
            scores = jnp.where(visible, scores, NEGATIVE)
            top = jnp.max(scores, axis=1, keepdims=True)
            weights = jnp.where(visible, jnp.exp2((scores - top) * scale), 0.0)
            total = jnp.sum(weights, axis=1, keepdims=True)
            mixed = jnp.dot(
                weights.astype(bf16), pairs[:, width:], preferred_element_type=f32
            )
            return (mixed / (total * gate)).astype(bf16)

        def spreads(chosen_rows):
            token = start + lax.broadcasted_iota(jnp.int32, (tok_rows, chosen), 0).astype(f32)
            return [
                jnp.where(chosen_rows[head : head + 1, :] == token, 1.0, 0.0).astype(bf16)
                for head in range(experts)
            ]

        def expert_write(spread, result):
            for head in range(experts):
                expert_ref[head] = jnp.dot(
                    spread[head],
                    result[head * chosen : (head + 1) * chosen],
                    preferred_element_type=f32,
                ).astype(bf16)

        @pl.when(first)
        def _():
            begin(3, 4, 5, 0, 2, 1, 6, 7)
            pl.semaphore_wait(barrier, 1)
            sent_k.start()
            sent_v.start()
            ready(3, 4, 5)
            chosen_rows, one_hot = choose()
            pick_pairs(one_hot)
            sent_picked.start()
            ready(0, 2, 1, 6, 7)
            split(k_in, 0, k_all)
            split(v_in, 2, v_all)
            split(q_in, 1, q_all)
            result = expert_result(*expert_query(one_hot), picked[...])
            staged(
                local_scores,
                lambda head, part, scores: finish(head, part, local_mix(head, part, scores)[1]),
            )
            expert_write(spreads(chosen_rows), result)
            dense_ref[...] = wide[1].astype(bf16)

        @pl.when(me == 1)
        def _():
            begin(0, 2, 1, 3, 4, 5, 6, 7)
            ready(0, 1, 2)
            split(k_in, 0, k_all)
            split(q_in, 1, q_all)
            split(v_in, 2, v_all)
            staged(
                local_scores,
                lambda head, part, scores: keep(head, part, *local_mix(head, part, scores)),
            )
            ready(3, 4, 5, 6, 7)
            chosen_rows, one_hot = choose()
            pick_pairs(one_hot)
            query, gate = expert_query(one_hot)
            spread = spreads(chosen_rows)
            sent_k.wait_recv()
            sent_v.wait_recv()
            sent_picked.wait_recv()
            split(k_far, 0, kf_all)
            split(v_far, 2, vf_all)
            result = expert_result(query, gate, picked[...] + picked_far[...])
            staged(
                far_scores,
                lambda head, part, scores: finish(head, part, far_mix(head, part, scores)),
            )
            expert_write(spread, result)
            dense_ref[...] = wide[1].astype(bf16)

        @pl.when(first)
        def _():
            sent_k.wait_send()
            sent_v.wait_send()
            sent_picked.wait_send()

    in_hbm = pl.BlockSpec(memory_space=pltpu.HBM)
    in_vmem = pl.BlockSpec(memory_space=pltpu.VMEM)
    flat = (tok_rows * heads, width)
    return pl.pallas_call(
        kernel,
        out_shape=(
            pltpu.VMEM(flat, bf16),
            pltpu.VMEM((experts, tok_rows, width), bf16),
        ),
        in_specs=[in_hbm] * 8,
        out_specs=(in_vmem, in_vmem),
        scratch_shapes=[pltpu.VMEM(flat, bf16)] * 5
        + [pltpu.VMEM((experts, tok_rows, width), bf16)] * 3
        + [
            pltpu.VMEM((3,) + flat, f32),
            pltpu.VMEM((heads, tok_rows, width), bf16),
            pltpu.VMEM((heads, tok_rows, width), bf16),
            pltpu.VMEM((heads, tok_rows, width), bf16),
            pltpu.VMEM((heads, tok_rows, width), bf16),
            pltpu.VMEM((heads, tok_rows, width), bf16),
            pltpu.VMEM((heads, tok_rows, 2 * width), f32),
            pltpu.VMEM((heads, tok_rows, width), f32),
            pltpu.VMEM((picks, 2 * width), bf16),
            pltpu.VMEM((picks, 2 * width), bf16),
            pltpu.VMEM((experts, tok_rows), bf16),
            pltpu.VMEM((experts, chosen), jnp.int32),
            pltpu.SemaphoreType.DMA((8,)),
            pltpu.SemaphoreType.DMA((3,)),
            pltpu.SemaphoreType.DMA((3,)),
        ],
        compiler_params=pltpu.CompilerParams(
            collective_id=0, has_side_effects=True, vmem_limit_bytes=32 * 1024 * 1024
        ),
    )


def write_out(dense, expert):
    def kernel(dense_ref, expert_ref, dense_out, expert_out, sems):
        copies = [
            pltpu.make_async_copy(expert_ref, expert_out, sems.at[0]),
            pltpu.make_async_copy(dense_ref, dense_out, sems.at[1]),
        ]
        for copy in copies:
            copy.start()
        for copy in copies:
            copy.wait()

    return pl.pallas_call(
        kernel,
        out_shape=tuple(
            pltpu.HBM(member.shape, member.dtype) for member in (dense, expert)
        ),
        in_specs=[pl.BlockSpec(memory_space=pltpu.VMEM)] * 2,
        out_specs=tuple([pl.BlockSpec(memory_space=pltpu.HBM)] * 2),
        scratch_shapes=[pltpu.SemaphoreType.DMA((2,))],
        compiler_params=pltpu.CompilerParams(vmem_limit_bytes=4 * 1024 * 1024),
    )(
        pltpu.with_memory_space_constraint(dense, pltpu.VMEM),
        pltpu.with_memory_space_constraint(expert, pltpu.VMEM),
    )


def local_pair(q_dense, k_dense, v_dense, q_expert, k_expert, v_expert, gate_logit, selection):
    tok_rows, heads, width = q_dense.shape
    experts, chosen = selection.shape
    call = nearest_pair(tok_rows, heads, width, experts, chosen)
    dense_out, expert_out = call(
        *(
            pltpu.with_memory_space_constraint(member, pltpu.HBM)
            for member in (
                q_dense.reshape(tok_rows * heads, width),
                k_dense.reshape(tok_rows * heads, width),
                v_dense.reshape(tok_rows * heads, width),
                jnp.transpose(q_expert, (1, 0, 2)),
                jnp.transpose(k_expert, (1, 0, 2)),
                jnp.transpose(v_expert, (1, 0, 2)),
                gate_logit,
                selection,
            )
        )
    )
    dense_out, expert_out = write_out(dense_out, expert_out)
    return (dense_out.reshape(tok_rows, heads, width), jnp.transpose(expert_out, (1, 0, 2)))


def solution(mesh):
    placed = (
        P(("dp", "seq"), "head", None),
        P(("dp", "seq"), "head", None),
        P(("dp", "seq"), "head", None),
        P(("dp", "seq"), "head", None),
        P(("dp", "seq"), "head", None),
        P(("dp", "seq"), "head", None),
        P("head", ("dp", "seq")),
        P("head", "dp"),
    )
    return jax.shard_map(
        local_pair if mesh.shape["seq"] == 2 else local,
        mesh=mesh,
        in_specs=placed,
        out_specs=(P(("dp", "seq"), "head", None), P(("dp", "seq"), "head", None)),
        check_vma=False,
    )
```
